256 devices in a mesh: inst: 32 (over x, z_lo, core), tp: 8 (over y, z_hi).
Axes of the slice: x: 4, y: 4, z: 8 (z_hi: 2, z_lo: 4; z = z_hi * 4 + z_lo), core: 2. Of those that a mesh axis runs over, the one named last changes fastest.
Arguments:
- queries: bfloat16 [4, 2048, 64, 128], P(None, 'inst', 'tp'), may hold values from -80 to 80
- new_keys: bfloat16 [4, 2048, 8, 128], P(None, 'inst', 'tp'), may hold values from -5 to 5
- new_values: bfloat16 [4, 2048, 8, 128], P(None, 'inst', 'tp'), may hold values from -6 to 6
- pool_keys: bfloat16 [6144, 8, 16, 128], P('inst', 'tp'), may hold values from -6 to 6
- pool_values: bfloat16 [6144, 8, 16, 128], P('inst', 'tp'), may hold values from -6 to 6
- prompt_keys: bfloat16 [6144, 8, 16, 128], P('inst', 'tp'), may hold values from -6 to 6
- prompt_values: bfloat16 [6144, 8, 16, 128], P('inst', 'tp'), may hold values from -6 to 6
- moved_keys: bfloat16 [3072, 8, 16, 128], P('inst', 'tp'), may hold values from -6 to 6
- moved_values: bfloat16 [3072, 8, 16, 128], P('inst', 'tp'), may hold values from -6 to 6
- prompt_dest: int32 [6144], P('inst'), may hold values from 0 to 31, as said below
- moved_dest: int32 [3072], P('inst'), may hold values from 0 to 31, as said below
- block_table: int32 [2048, 48], P('inst'), may hold values from 0 to 767, as said below
- context_len: int32 [2048], P('inst'), may hold values from 1 to 768, as said below
- out_weight: bfloat16 [8192, 4096], P('tp'), may hold values from -0.25 to 0.25
Outputs:
- mixed: bfloat16 [4, 2048, 4096], P(None, 'inst', 'tp')
The draws below stay inside these ranges and needn't reach their ends.
Inputs may be any that keep to these rules, and one draw needn't show every extreme that they name: `prompt_dest`: entry s * 192 + j names the instance that receives prompt page j of instance s. No instance receives more than 12 pages from one source; in every draw every source sends exactly 12 pages to some instance. `moved_dest`: entry s * 96 + j names the new owner of migrating page j of instance s. No instance receives more than 6 pages from one source; in every draw every source sends exactly 6 pages to some instance. `block_table`: local page ids of the instance that holds the row. Only filled arrival slots are named; over the rows of an instance each page is named at most once in the first ceil(context_len / 16) entries of a row; later entries hold 0 and are not read. `context_len`: some sequence of every instance has exactly 768 cached tokens.
All inputs are finite; a program needn't handle non-finite values.
Results may differ from the reference program's by a relative error of at most 0.0057.
Values may be sent and summed in bfloat16 or wider, within the bound.
No kernel may reach another device: no remote copies, remote signals or barrier semaphores. Data moves between devices by JAX's collectives and lax.ppermute only.
A program may use at most 256 MiB of HBM per device.

```python
import jax
import jax.numpy as jnp
from jax import lax

H = 64
KVH = 8
DH = 128
DW = 4096
PAGE = 16
STEPS = 4
MAXP = 48
ROWS = 64
POOL = 192
OUT = 192
MIG = 96
RTOT = 2048
POOL_ALL = 6144
OUT_ALL = 6144
MIG_ALL = 3072
PCAP = 12
MCAP = 6
N_INST = 32


def page_routes(key, salt, per, capacity):
    key = jax.random.fold_in(key, salt)
    first, second, third = jax.random.split(key, 3)
    slots = N_INST * capacity
    owner = jnp.arange(slots, dtype=jnp.int32) // capacity
    heavy = jax.random.randint(first, (N_INST,), 0, N_INST)
    tilt = jax.random.randint(second, (N_INST, N_INST), 0, 1024)
    noise = jax.random.randint(third, (N_INST, slots), 0, 1024)
    score = tilt[:, owner] + noise + jnp.where(owner[None, :] == heavy[:, None], 4096, 0)
    score = score * slots + jnp.arange(slots, dtype=jnp.int32)[None, :]
    chosen = lax.top_k(score, per)[1]
    return (chosen // capacity).astype(jnp.int32)


def prompt_routes(key):
    return page_routes(key, 101, OUT, 2 * OUT // N_INST)


def moved_routes(key):
    return page_routes(key, 202, MIG, 2 * MIG // N_INST)


def page_layout(key):
    prompt_cap = 2 * OUT // N_INST
    moved_cap = 2 * MIG // N_INST
    instances = jnp.arange(N_INST, dtype=jnp.int32)
    prompt_counts = jnp.sum((prompt_routes(key)[:, :, None] == instances[None, None, :]).astype(jnp.int32), axis=1)
    moved_counts = jnp.sum((moved_routes(key)[:, :, None] == instances[None, None, :]).astype(jnp.int32), axis=1)
    order_key, weight_key, tail_key = jax.random.split(jax.random.fold_in(key, 303), 3)
    local = POOL + N_INST * prompt_cap + N_INST * moved_cap
    prompt_rank = jnp.tile(jnp.arange(prompt_cap, dtype=jnp.int32), N_INST)
    prompt_source = jnp.repeat(instances, prompt_cap)
    moved_rank = jnp.tile(jnp.arange(moved_cap, dtype=jnp.int32), N_INST)
    moved_source = jnp.repeat(instances, moved_cap)
    rows = jnp.arange(ROWS, dtype=jnp.int32)
    column = jnp.arange(MAXP, dtype=jnp.int32)

    def one(index, noise_key, row_key, end_key):
        valid = jnp.concatenate([jnp.ones((POOL,), jnp.int32), (prompt_rank < prompt_counts[prompt_source, index]).astype(jnp.int32), (moved_rank < moved_counts[moved_source, index]).astype(jnp.int32)])
        noise = jax.random.randint(noise_key, (local,), 0, 4096)
        score = valid * (1 << 30) + noise * local + jnp.arange(local, dtype=jnp.int32)
        order = jnp.argsort(-score).astype(jnp.int32)
        count = jnp.sum(valid)
        weights = jax.random.randint(row_key, (ROWS,), 1, 5)
        spare = count - MAXP - (ROWS - 1)
        share = spare * weights // jnp.sum(jnp.where(rows > 0, weights, 0))
        lengths = jnp.where(rows == 0, MAXP, 1 + jnp.minimum(MAXP - 1, share))
        starts = jnp.cumsum(lengths).astype(jnp.int32) - lengths
        picked = order[jnp.minimum(starts[:, None] + column[None, :], local - 1)]
        table = jnp.where(column[None, :] < lengths[:, None], picked, 0)
        tail = jax.random.randint(end_key, (ROWS,), 1, PAGE + 1)
        tail = jnp.where(rows == 0, PAGE, tail)
        return (table.astype(jnp.int32), ((lengths - 1) * PAGE + tail).astype(jnp.int32))
    tables, contexts = jax.vmap(one)(instances, jax.random.split(order_key, N_INST), jax.random.split(weight_key, N_INST), jax.random.split(tail_key, N_INST))
    return (tables.reshape(N_INST * ROWS, MAXP), contexts.reshape(N_INST * ROWS))


def shared_keys(key):
    base = jax.random.normal(jax.random.fold_in(key, 404), (STEPS, N_INST * ROWS, KVH, DH), jnp.float32)
    return jnp.clip(base, -4.0, 4.0)


def draw_prompt_dest(key, part):
    routes = prompt_routes(key)
    return routes.reshape(-1)


def draw_moved_dest(key, part):
    routes = moved_routes(key)
    return routes.reshape(-1)


def draw_block_table(key, part):
    table, contexts = page_layout(key)
    return table


def draw_context_len(key, part):
    table, contexts = page_layout(key)
    return contexts


def draw_new_keys(key, part):
    shared = shared_keys(key)
    key = jax.random.fold_in(key, 5)
    noise = jnp.clip(jax.random.normal(key, shared.shape, jnp.float32), -4.0, 4.0)
    return noise.astype(jnp.bfloat16)


def draw_queries(key, part):
    key = jax.random.fold_in(key, 6)
    shape = (STEPS, N_INST * ROWS, H, DH)
    return jnp.clip(1.5 * jax.random.normal(key, shape, jnp.float32), -9.0, 9.0).astype(jnp.bfloat16)


def level_of(stream_key, shape, shards, least, high):
    def one(dim, parts):
        steps = jax.random.uniform(jax.random.fold_in(jax.random.fold_in(stream_key, 6), dim), (parts,), jnp.float32, least / len(shards), high / len(shards))
        return jnp.repeat(jnp.exp(steps), shape[dim] // parts).reshape((-1,) + (1,) * (len(shape) - dim - 1))

    factor_of = one(*shards[0])
    for cut in shards[1:]:
        factor_of = factor_of * one(*cut)
    return factor_of


def bell_draw(rng, dims, width, most, shards=(), kind=jnp.bfloat16):
    drawn = jax.random.normal(rng, dims, jnp.float32) * width
    if len(shards) > 0:
        drawn = level_of(rng, dims, shards, -0.22, 0.18) * drawn
    return jnp.clip(drawn, min=-most, max=most).astype(kind)


def setup_inputs(seed: int = 0) -> dict:
    key_list = jax.random.split(jax.random.key(seed), 15)
    return {
        "queries": draw_queries(jax.random.fold_in(key_list[14], 71), 0),
        "new_keys": draw_new_keys(jax.random.fold_in(key_list[14], 71), 0),
        "new_values": bell_draw(key_list[2], (STEPS, RTOT, KVH, DH), 1.0, 6.0, ((1, 32), (2, 8))),
        "pool_keys": bell_draw(key_list[3], (POOL_ALL, KVH, PAGE, DH), 1.0, 6.0, ((0, 32), (1, 8))),
        "pool_values": bell_draw(key_list[4], (POOL_ALL, KVH, PAGE, DH), 1.0, 6.0, ((0, 32), (1, 8))),
        "prompt_keys": bell_draw(key_list[5], (OUT_ALL, KVH, PAGE, DH), 1.0, 6.0, ((0, 32), (1, 8))),
        "prompt_values": bell_draw(key_list[6], (OUT_ALL, KVH, PAGE, DH), 1.0, 6.0, ((0, 32), (1, 8))),
        "moved_keys": bell_draw(key_list[7], (MIG_ALL, KVH, PAGE, DH), 1.0, 6.0, ((0, 32), (1, 8))),
        "moved_values": bell_draw(key_list[8], (MIG_ALL, KVH, PAGE, DH), 1.0, 6.0, ((0, 32), (1, 8))),
        "prompt_dest": draw_prompt_dest(jax.random.fold_in(key_list[14], 71), 0),
        "moved_dest": draw_moved_dest(jax.random.fold_in(key_list[14], 71), 0),
        "block_table": draw_block_table(jax.random.fold_in(key_list[14], 71), 0),
        "context_len": draw_context_len(jax.random.fold_in(key_list[14], 71), 0),
        "out_weight": bell_draw(key_list[13], (H * DH, DW), (H * DH // 16) ** -0.5, 0.25, ((0, 8),)),
    }


def slot_pages(destination, capacity, index, base):
    sources, per = destination.shape
    hits = (destination == index).astype(jnp.int32)
    rank = (jnp.cumsum(hits, axis=1) - 1).astype(jnp.int32)
    slot = jnp.where(hits > 0, jnp.arange(sources, dtype=jnp.int32)[:, None] * capacity + rank, sources * capacity)
    page_ids = base + jnp.arange(sources * per, dtype=jnp.int32).reshape(sources, per)
    filled = jnp.zeros((sources * capacity + 1,), jnp.int32).at[slot.reshape(-1)].set(page_ids.reshape(-1))
    return filled[:sources * capacity]


def attention_weights(query_block, keys_block, fresh_keys, lengths):
    steps_count = query_block.shape[0]
    scale = DH ** -0.5
    cached = jnp.einsum("srkgd,rpkod->srkgpo", query_block, keys_block) * scale
    cached = cached.reshape(cached.shape[:4] + (-1,))
    position = jnp.arange(cached.shape[-1], dtype=jnp.int32)
    visible = position[None, :] < lengths[:, None]
    cached = jnp.where(visible[None, :, None, None, :], cached, -jnp.inf)
    recent = jnp.einsum("srkgd,urkd->srkgu", query_block, fresh_keys) * scale
    causal = jnp.arange(steps_count, dtype=jnp.int32)[None, :] <= jnp.arange(steps_count, dtype=jnp.int32)[:, None]
    recent = jnp.where(causal[:, None, None, None, :], recent, -jnp.inf)
    largest = jnp.maximum(jnp.max(cached, axis=-1), jnp.max(recent, axis=-1))
    cached_exp = jnp.exp(cached - largest[..., None])
    recent_exp = jnp.exp(recent - largest[..., None])
    total = jnp.sum(cached_exp, axis=-1) + jnp.sum(recent_exp, axis=-1)
    cached_w = (cached_exp / total[..., None]).astype(jnp.bfloat16)
    recent_w = (recent_exp / total[..., None]).astype(jnp.bfloat16)
    return cached_w, recent_w


def reference(queries, new_keys, new_values, pool_keys, pool_values, prompt_keys, prompt_values, moved_keys, moved_values, prompt_dest, moved_dest, block_table, context_len, out_weight):
    all_keys = jnp.concatenate([pool_keys, prompt_keys, moved_keys], axis=0)
    all_values = jnp.concatenate([pool_values, prompt_values, moved_values], axis=0)
    prompt_grid = prompt_dest.reshape(N_INST, OUT)
    moved_grid = moved_dest.reshape(N_INST, MIG)
    groups = H // KVH

    def instance(index):
        first = index * ROWS
        store_ids = jnp.concatenate([
            index * POOL + jnp.arange(POOL, dtype=jnp.int32),
            slot_pages(prompt_grid, PCAP, index, N_INST * POOL),
            slot_pages(moved_grid, MCAP, index, N_INST * POOL + N_INST * OUT)], axis=0)
        table = lax.dynamic_slice_in_dim(block_table, first, ROWS, 0)
        lengths = lax.dynamic_slice_in_dim(context_len, first, ROWS, 0)
        global_ids = jnp.take(store_ids, table, axis=0)
        query_block = lax.dynamic_slice_in_dim(queries, first, ROWS, 1).astype(jnp.float32)
        query_block = query_block.reshape(STEPS, ROWS, KVH, groups, DH)
        fresh_keys = lax.dynamic_slice_in_dim(new_keys, first, ROWS, 1).astype(jnp.float32)
        fresh_values = lax.dynamic_slice_in_dim(new_values, first, ROWS, 1).astype(jnp.float32)
        keys_block = jnp.take(all_keys, global_ids, axis=0).astype(jnp.float32)
        values_block = jnp.take(all_values, global_ids, axis=0).astype(jnp.float32)
        cached_w, recent_w = attention_weights(query_block, keys_block, fresh_keys, lengths)
        cached_w = cached_w.reshape(cached_w.shape[:4] + (MAXP, PAGE)).astype(jnp.float32)
        heads = jnp.einsum("srkgpo,rpkod->srkgd", cached_w, values_block)
        heads = heads + jnp.einsum("srkgu,urkd->srkgd", recent_w.astype(jnp.float32), fresh_values)
        return heads.astype(jnp.bfloat16).reshape(STEPS, ROWS, H * DH)

    heads_out = lax.map(instance, jnp.arange(N_INST, dtype=jnp.int32))
    heads_out = jnp.transpose(heads_out, (1, 0, 2, 3)).reshape(STEPS * N_INST * ROWS, H * DH)
    mixed = jnp.dot(heads_out, out_weight, preferred_element_type=jnp.float32).astype(jnp.bfloat16)
    return mixed.reshape(STEPS, N_INST * ROWS, DW)
```

```python
import functools

import jax
import jax.numpy as jnp
from jax import lax
from jax.experimental import pallas as pl
from jax.experimental.pallas import tpu as pltpu
from jax.sharding import Mesh, PartitionSpec as P

NAMES = ("ix", "izh", "izl", "ic", "ty", "tz")
SIZES = (4, 2, 2, 2, 4, 2)
INST = ("ix", "izh", "izl", "ic")
HALF = ("ix", "izl", "ic")
TP = ("ty", "tz")

N_INST = 32
N_HALF = 16
STEPS, ROWS, GROUPS, DH = 4, 64, 8, 128
QROWS = STEPS * GROUPS
PAGE, MAXP = 16, 48
POOL, OUT, MIG = 192, 192, 96
PCAP, MCAP = 12, 6
SLOTS = PCAP + MCAP
RECV = N_HALF * SLOTS
CHUNK_PAGES = 16
CHUNK = CHUNK_PAGES * PAGE
WIDE_CHUNKS = 4
POSITIONS = CHUNK_PAGES * WIDE_CHUNKS
UNROLL = 8
SCALE = DH ** -0.5
VMEM_LIMIT = 40 * 1024 * 1024


def pack_kernel(pdest, mdest, pk, pv, mk, mv, send, count):
    def clear(i, carry):
        count[i] = 0
        return carry

    def place(dest, keys, values, first, j):
        d = dest[j]
        k = count[d]
        count[d] = k + 1
        block = (d >> 3) * 8 + (d & 3) * 2 + ((d >> 2) & 1)
        slot = block * SLOTS + first + k
        send[slot, 0] = keys[j]
        send[slot, 1] = values[j]

    def prompt(j, carry):
        place(pdest, pk, pv, 0, j)
        return carry

    def moved(j, carry):
        place(mdest, mk, mv, PCAP, j)
        return carry

    lax.fori_loop(0, N_INST, clear, 0)
    lax.fori_loop(0, OUT, prompt, 0, unroll=4)
    lax.fori_loop(0, N_INST, clear, 0)
    lax.fori_loop(0, MIG, moved, 0, unroll=4)


def pack(pdest, mdest, pk, pv, mk, mv):
    smem = pl.BlockSpec(memory_space=pltpu.SMEM)
    vmem = pl.BlockSpec(memory_space=pltpu.VMEM)
    return pl.pallas_call(
        pack_kernel,
        out_shape=jax.ShapeDtypeStruct((N_INST * SLOTS, 2, PAGE, DH), jnp.bfloat16),
        in_specs=[smem, smem, vmem, vmem, vmem, vmem],
        out_specs=vmem,
        scratch_shapes=[pltpu.SMEM((N_INST,), jnp.int32)],
        compiler_params=pltpu.CompilerParams(vmem_limit_bytes=VMEM_LIMIT),
        name="pack_pages",
    )(pdest, mdest, pk, pv, mk, mv)


def attend_kernel(own, half, ctx, idx, bias, q, recv, *refs):
    if own:
        pool_k, pool_v, fresh, out, lse, kv, acc, sem = refs
    else:
        out, lse, kv, acc, sem = refs
    first = 1 + POOL + ROWS if own else 1
    copies = [
        pltpu.make_async_copy(recv.at[g, half[0]], kv.at[pl.ds(first + g * SLOTS, SLOTS)], sem)
        for g in range(N_HALF)
    ]
    if own:
        copies.append(pltpu.make_async_copy(pool_k, kv.at[pl.ds(1, POOL), 0], sem))
        copies.append(pltpu.make_async_copy(pool_v, kv.at[pl.ds(1, POOL), 1], sem))
        copies.append(pltpu.make_async_copy(fresh, kv.at[pl.ds(1 + POOL, ROWS)], sem))
    for copy in copies:
        copy.start()
    kv[0] = jnp.zeros((2, PAGE, DH), jnp.bfloat16)
    for copy in copies:
        copy.wait()

    lane = lax.broadcasted_iota(jnp.int32, (QROWS, CHUNK), 1)
    step = lax.broadcasted_iota(jnp.int32, (QROWS, CHUNK), 0) // GROUPS
    causal = jnp.where((lane > step) & (lane < PAGE), -jnp.inf, 0.0).astype(jnp.float32)
    column = lax.broadcasted_iota(jnp.int32, (QROWS, 128), 1)

    def chunk_pages(r, c):
        return [idx[r * POSITIONS + c * CHUNK_PAGES + p] for p in range(CHUNK_PAGES)]

    def chunk_scores(r, c, pages):
        keys = jnp.concatenate([kv[i, 0] for i in pages], axis=0)
        s = lax.dot_general(q[r], keys, (((1,), (1,)), ((), ())), preferred_element_type=jnp.float32)
        s = s * SCALE + bias[pl.ds(r, 1), pl.ds(c * CHUNK, CHUNK)]
        return s + causal if own and c == 0 else s

    def chunk_out(weights, pages):
        values = jnp.concatenate([kv[i, 1] for i in pages], axis=0)
        return jnp.dot(weights.astype(jnp.bfloat16), values, preferred_element_type=jnp.float32)

    def finish(r, m, total, product):
        safe = jnp.maximum(total, 1e-30)
        acc[pl.ds(r, QROWS, stride=ROWS), :] = product / safe
        return jnp.where(total > 0.0, m + jnp.log(safe), -1e30)

    def narrow(i, stats):
        for u in range(UNROLL):
            r = i * UNROLL + u
            pages = chunk_pages(r, 0)
            s = chunk_scores(r, 0, pages)
            m = jnp.maximum(jnp.max(s, axis=1, keepdims=True), -1e30)
            e = jnp.exp(s - m)
            total = jnp.sum(e, axis=1, keepdims=True)
            stats = jnp.where(column == r, finish(r, m, total, chunk_out(e, pages)), stats)
        return stats

    lse[...] = lax.fori_loop(0, ROWS // UNROLL, narrow, jnp.zeros((QROWS, 128), jnp.float32))

    def wide(r, carry):
        @pl.when(ctx[r] > (CHUNK_PAGES - 1) * PAGE)
        def _():
            scores = [chunk_scores(r, c, chunk_pages(r, c)) for c in range(WIDE_CHUNKS)]
            m = jnp.full((QROWS, 1), -1e30, jnp.float32)
            for s in scores:
                m = jnp.maximum(m, jnp.max(s, axis=1, keepdims=True))
            total = jnp.zeros((QROWS, 1), jnp.float32)
            product = jnp.zeros((QROWS, DH), jnp.float32)
            for c, s in enumerate(scores):
                e = jnp.exp(s - m)
                total = total + jnp.sum(e, axis=1, keepdims=True)
                product = product + chunk_out(e, chunk_pages(r, c))
            lse[...] = jnp.where(column == r, finish(r, m, total, product), lse[...])

        return carry

    lax.fori_loop(0, ROWS, wide, 0)
    out[...] = acc[...].astype(out.dtype)


def attend(own, half, ctx, idx, bias, q, recv, *local):
    smem = pl.BlockSpec(memory_space=pltpu.SMEM)
    vmem = pl.BlockSpec(memory_space=pltpu.VMEM)
    hbm = pl.BlockSpec(memory_space=pl.ANY)
    pages = 1 + RECV + (POOL + ROWS if own else 0)
    dtype = jnp.float32 if own else jnp.bfloat16
    return pl.pallas_call(
        functools.partial(attend_kernel, own),
        out_shape=(
            jax.ShapeDtypeStruct((QROWS * ROWS, DH), dtype),
            jax.ShapeDtypeStruct((QROWS, 128), jnp.float32),
        ),
        in_specs=[smem, smem, smem, vmem, vmem, hbm] + [hbm] * len(local),
        out_specs=(vmem, vmem),
        scratch_shapes=[
            pltpu.VMEM((pages, 2, PAGE, DH), jnp.bfloat16),
            pltpu.VMEM((QROWS * ROWS, DH), jnp.float32),
            pltpu.SemaphoreType.DMA,
        ],
        compiler_params=pltpu.CompilerParams(vmem_limit_bytes=VMEM_LIMIT),
        cost_estimate=pl.CostEstimate(flops=10**9, bytes_accessed=8 * 10**6, transcendentals=10**6),
        name="attend_own" if own else "attend_mirror",
    )(half, ctx, idx, bias, q, recv, *local)


def mix_kernel(o1, lse1, o2, lse2, weight, out, heads):
    @pl.when(pl.program_id(0) == 0)
    def _():
        top = jnp.maximum(lse1[...], lse2[...])
        e1 = jnp.exp(lse1[...] - top)
        e2 = jnp.exp(lse2[...] - top)
        inverse = 1.0 / (e1 + e2)
        f1 = (e1 * inverse).T
        f2 = (e2 * inverse).T
        for j in range(QROWS):
            t, h = j // GROUPS, j % GROUPS
            rows = pl.ds(j * ROWS, ROWS)
            merged = f1[:ROWS, j : j + 1] * o1[rows, :] + f2[:ROWS, j : j + 1] * o2[rows, :].astype(jnp.float32)
            heads[pl.ds(t * ROWS, ROWS), pl.ds(h * DH, DH)] = merged.astype(jnp.bfloat16)

    out[0] = jnp.dot(heads[...], weight[...], preferred_element_type=jnp.float32).astype(jnp.bfloat16)


def mix(o1, lse1, o2, lse2, weight):
    depth, width = weight.shape
    block = width // 8
    whole = lambda shape: pl.BlockSpec(shape, lambda n: (0, 0))
    return pl.pallas_call(
        mix_kernel,
        grid=(8,),
        out_shape=jax.ShapeDtypeStruct((8, STEPS * ROWS, block), jnp.bfloat16),
        in_specs=[
            whole(o1.shape),
            whole(lse1.shape),
            whole(o2.shape),
            whole(lse2.shape),
            pl.BlockSpec((depth, block), lambda n: (0, n)),
        ],
        out_specs=pl.BlockSpec((1, STEPS * ROWS, block), lambda n: (n, 0, 0)),
        scratch_shapes=[pltpu.VMEM((STEPS * ROWS, depth), jnp.bfloat16)],
        compiler_params=pltpu.CompilerParams(vmem_limit_bytes=VMEM_LIMIT),
        name="merge_and_project",
    )(o1, lse1, o2, lse2, weight)


def routes(own, table, lengths, half):
    column = jnp.arange(MAXP, dtype=jnp.int32)[None, :]
    valid = column * PAGE < lengths[:, None]
    prompt = table < POOL + N_INST * PCAP
    px, mx = table - POOL, table - (POOL + N_INST * PCAP)
    source = jnp.where(prompt, px // PCAP, mx // MCAP)
    rank = jnp.where(prompt, px % PCAP, PCAP + mx % MCAP)
    group = (source >> 3) * 4 + (source & 3)
    arrived = (table >= POOL) & (((source >> 2) & 1) == half)
    if own:
        place = jnp.where(table < POOL, 1 + table, 1 + POOL + ROWS + group * SLOTS + rank)
        here = valid & (arrived | (table < POOL))
        fresh = 1 + POOL + jnp.arange(ROWS, dtype=jnp.int32)[:, None]
    else:
        place = 1 + group * SLOTS + rank
        here = valid & arrived
        fresh = jnp.zeros((ROWS, 1), jnp.int32)
    spare = POSITIONS - 1 - MAXP
    idx = jnp.concatenate([fresh, jnp.where(here, place, 0), jnp.zeros((ROWS, spare), jnp.int32)], axis=1)
    token = (column * PAGE)[:, :, None] + jnp.arange(PAGE, dtype=jnp.int32)[None, None, :]
    seen = (here[:, :, None] & (token < lengths[:, None, None])).reshape(ROWS, MAXP * PAGE)
    seen = jnp.concatenate(
        [jnp.full((ROWS, PAGE), own), seen, jnp.zeros((ROWS, spare * PAGE), jnp.bool_)], axis=1
    )
    return idx.reshape(-1), jnp.where(seen, 0.0, -jnp.inf).astype(jnp.float32)


def by_row(queries):
    return queries.transpose(1, 0, 2, 3).reshape(ROWS, QROWS, DH)


def per_device(
    queries,
    new_keys,
    new_values,
    pool_keys,
    pool_values,
    prompt_keys,
    prompt_values,
    moved_keys,
    moved_values,
    prompt_dest,
    moved_dest,
    block_table,
    context_len,
    out_weight,
):
    page = lambda x: x.reshape(x.shape[0], PAGE, DH)
    swap = [(0, 1), (1, 0)]
    half = lax.axis_index("izh")

    send = pack(
        prompt_dest, moved_dest, page(prompt_keys), page(prompt_values), page(moved_keys), page(moved_values)
    )
    send = send.reshape(N_HALF, 2 * SLOTS, 2, PAGE, DH)
    recv = lax.all_to_all(send, HALF, split_axis=0, concat_axis=0, tiled=True)
    recv = recv.reshape(N_HALF, 2, SLOTS, 2, PAGE, DH)

    tables = jnp.concatenate([block_table, context_len[:, None]], axis=1)
    mirror_q = lax.ppermute(queries, "izh", swap)
    mirror_tables = lax.ppermute(tables, "izh", swap)
    mirror_len = mirror_tables[:, MAXP]

    idx2, bias2 = routes(False, mirror_tables[:, :MAXP], mirror_len, half)
    o2, lse2 = attend(False, (1 - half)[None], mirror_len, idx2, bias2, by_row(mirror_q), recv)
    o2 = lax.ppermute(o2, "izh", swap)
    lse2 = lax.ppermute(lse2, "izh", swap)

    fresh = jnp.stack([new_keys, new_values], axis=0).reshape(2, STEPS, ROWS, DH).transpose(2, 0, 1, 3)
    fresh = jnp.pad(fresh, ((0, 0), (0, 0), (0, PAGE - STEPS), (0, 0)))
    idx1, bias1 = routes(True, block_table, context_len, half)
    o1, lse1 = attend(
        True, half[None], context_len, idx1, bias1, by_row(queries), recv, page(pool_keys), page(pool_values), fresh
    )

    terms = mix(o1, lse1, o2, lse2, out_weight)
    terms = terms.reshape(4, 2, STEPS * ROWS, -1)
    got = lax.all_to_all(terms, "ty", split_axis=0, concat_axis=0, tiled=True)
    column = got.astype(jnp.float32).sum(axis=0)
    side = lax.axis_index("tz")
    mine = jnp.where(side == 0, column[0], column[1])
    other = jnp.where(side == 0, column[1], column[0]).astype(jnp.bfloat16)
    other = lax.ppermute(other, "tz", swap)
    mixed = (mine + other.astype(jnp.float32)).astype(jnp.bfloat16)
    return mixed.reshape(STEPS, ROWS, -1)


def solution(mesh):
    fine = Mesh(mesh.devices.reshape(SIZES), NAMES)
    in_specs = (
        P(None, INST, TP, None),
        P(None, INST, TP, None),
        P(None, INST, TP, None),
        P(INST, TP, None, None),
        P(INST, TP, None, None),
        P(INST, TP, None, None),
        P(INST, TP, None, None),
        P(INST, TP, None, None),
        P(INST, TP, None, None),
        P(INST),
        P(INST),
        P(INST, None),
        P(INST),
        P(TP, None),
    )
    return jax.shard_map(
        per_device, mesh=fine, in_specs=in_specs, out_specs=P(None, INST, TP), check_vma=False
    )
```

```python
import functools

import jax
import jax.numpy as jnp
from jax import lax
from jax.experimental import pallas as pl
from jax.experimental.pallas import tpu as pltpu
from jax.sharding import Mesh, PartitionSpec as P

NAMES = ("ix", "izh", "izl", "ic", "ty", "tz")
SIZES = (4, 2, 2, 2, 4, 2)
INST = ("ix", "izh", "izl", "ic")
HALF = ("ix", "izl", "ic")
TP = ("ty", "tz")

N_INST = 32
N_HALF = 16
STEPS, ROWS, GROUPS, DH = 4, 64, 8, 128
QROWS = STEPS * GROUPS
PAGE, MAXP = 16, 48
POOL, OUT, MIG = 192, 192, 96
PCAP, MCAP = 12, 6
SLOTS = PCAP + MCAP
RECV = N_HALF * SLOTS
NARROW = 8
WIDE = 16
WIDE_CHUNKS = 4
UNROLL = 2
POSITIONS = WIDE * WIDE_CHUNKS
TEAM = 4
TEAMS = ROWS // TEAM
LANES = TEAM * QROWS
SCALE = DH ** -0.5
VMEM_LIMIT = 60 * 1024 * 1024

SMEM = pl.BlockSpec(memory_space=pltpu.SMEM)
VMEM = pl.BlockSpec(memory_space=pltpu.VMEM)
ANY = pl.BlockSpec(memory_space=pl.ANY)
PARAMS = pltpu.CompilerParams(vmem_limit_bytes=VMEM_LIMIT)


def pack_kernel(half, pdest, mdest, pk, pv, mk, mv, far, near, pages, send, count, sems, out_sems):
    loads = [
        pltpu.make_async_copy(pk, pages.at[pl.ds(0, OUT), 0], sems.at[0]),
        pltpu.make_async_copy(pv, pages.at[pl.ds(0, OUT), 1], sems.at[1]),
        pltpu.make_async_copy(mk, pages.at[pl.ds(OUT, MIG), 0], sems.at[2]),
        pltpu.make_async_copy(mv, pages.at[pl.ds(OUT, MIG), 1], sems.at[3]),
    ]
    for load in loads:
        load.start()
    mine = half[0]

    def clear(i, carry):
        count[i] = 0
        return carry

    def place(dest, first, origin, j):
        d = dest[j]
        k = count[d]
        count[d] = k + 1
        group = (d >> 3) * 4 + (d & 3)
        here = jnp.where(((d >> 2) & 1) == mine, RECV, 0)
        slot = here + group * SLOTS + first + k
        send[slot] = pages[origin + j]

    def prompt(j, carry):
        place(pdest, 0, 0, j)
        return carry

    def moved(j, carry):
        place(mdest, PCAP, OUT, j)
        return carry

    lax.fori_loop(0, N_INST, clear, 0)
    loads[0].wait()
    loads[1].wait()
    lax.fori_loop(0, OUT, prompt, 0, unroll=4)
    lax.fori_loop(0, N_INST, clear, 0)
    loads[2].wait()
    loads[3].wait()
    lax.fori_loop(0, MIG, moved, 0, unroll=4)
    stores = [
        pltpu.make_async_copy(send.at[pl.ds(0, RECV)], far, out_sems.at[0]),
        pltpu.make_async_copy(send.at[pl.ds(RECV, RECV)], near, out_sems.at[1]),
    ]
    for store in stores:
        store.start()
    for store in stores:
        store.wait()


def pack(half, pdest, mdest, pk, pv, mk, mv):
    shape = jax.ShapeDtypeStruct((RECV, 2, PAGE, DH), jnp.bfloat16)
    return pl.pallas_call(
        pack_kernel,
        out_shape=(shape, shape),
        in_specs=[SMEM, SMEM, SMEM, ANY, ANY, ANY, ANY],
        out_specs=(ANY, ANY),
        scratch_shapes=[
            pltpu.VMEM((OUT + MIG, 2, PAGE, DH), jnp.bfloat16),
            pltpu.VMEM((2 * RECV, 2, PAGE, DH), jnp.bfloat16),
            pltpu.SMEM((N_INST,), jnp.int32),
            pltpu.SemaphoreType.DMA((4,)),
            pltpu.SemaphoreType.DMA((2,)),
        ],
        compiler_params=PARAMS,
        name="pack_pages",
    )(half, pdest, mdest, pk, pv, mk, mv)


def attention(fresh, idx, count, tokens, q, kv, out, lse, scores):
    lane = lax.broadcasted_iota(jnp.int32, (1, LANES), 1)
    team_row = lane // QROWS
    step = (lane % QROWS) // GROUPS

    def load(r, first, n, which):
        return [kv[idx[r * POSITIONS + first + p], which] for p in range(n)]

    def mask(s, first, limit):
        token = lax.broadcasted_iota(jnp.int32, s.shape, 0) + first
        seen = token < limit
        if fresh:
            seen = token < jnp.where(token < PAGE, step + 1, limit)
        return jnp.where(seen, s * SCALE, -jnp.inf)

    def dot_nt(a, b):
        return lax.dot_general(a, b, (((1,), (1,)), ((), ())), preferred_element_type=jnp.float32)

    def narrow(g):
        width = NARROW * PAGE
        rows = [g * TEAM + i for i in range(TEAM)]
        keys = jnp.concatenate([k for r in rows for k in load(r, 0, NARROW, 0)], axis=0)
        s_all = dot_nt(keys, q[g])
        s = s_all[:width]
        limit = jnp.full((1, LANES), tokens[rows[0]], jnp.int32)
        owner = lax.broadcasted_iota(jnp.int32, (width, LANES), 1) // QROWS
        for i in range(1, TEAM):
            s = jnp.where(owner == i, s_all[i * width : (i + 1) * width], s)
            limit = jnp.where(team_row == i, tokens[rows[i]], limit)
        s = mask(s, 0, limit)
        m = jnp.maximum(jnp.max(s, axis=0, keepdims=True), -1e30)
        e = jnp.exp(s - m)
        total = jnp.sum(e, axis=0, keepdims=True)
        safe = jnp.maximum(total, 1e-30)
        lse[pl.ds(g, 1), :] = jnp.where(total > 0.0, m + jnp.log(safe), -1e30)
        weights = (e * (1.0 / safe)).T.astype(jnp.bfloat16)
        for i in range(TEAM):
            values = jnp.concatenate(load(rows[i], 0, NARROW, 1), axis=0)
            part = weights[i * QROWS : (i + 1) * QROWS]
            first = pl.multiple_of(g * LANES + i * QROWS, QROWS)
            out[pl.ds(first, QROWS), :] = jnp.dot(part, values, preferred_element_type=jnp.float32)

    def narrow_body(n, carry):
        for u in range(UNROLL):
            narrow(n * UNROLL + u)
        return carry

    lax.fori_loop(0, TEAMS // UNROLL, narrow_body, 0)

    def wide(r):
        width = WIDE * PAGE
        chunks = (count[r] + WIDE - 1) // WIDE
        g, i = r // TEAM, r % TEAM

        def first_pass(c, m):
            keys = jnp.concatenate(load(r, c * WIDE, WIDE, 0), axis=0)
            s = mask(dot_nt(keys, q[g]), c * width, tokens[r])
            scores[c] = s
            return jnp.maximum(m, jnp.max(s, axis=0, keepdims=True))

        m = lax.fori_loop(0, chunks, first_pass, jnp.full((1, LANES), -1e30, jnp.float32))

        def second_pass(c, total):
            e = jnp.exp(scores[c] - m)
            scores[c] = e
            return total + jnp.sum(e, axis=0, keepdims=True)

        total = lax.fori_loop(0, chunks, second_pass, jnp.zeros((1, LANES), jnp.float32))
        safe = jnp.maximum(total, 1e-30)
        inverse = 1.0 / safe

        def third_pass(c, product):
            weights = (scores[c] * inverse).T.astype(jnp.bfloat16)
            values = jnp.concatenate(load(r, c * WIDE, WIDE, 1), axis=0)
            return product + jnp.dot(weights, values, preferred_element_type=jnp.float32)

        product = lax.fori_loop(0, chunks, third_pass, jnp.zeros((LANES, DH), jnp.float32))
        rows = pl.ds(pl.multiple_of(g * LANES, LANES), LANES)
        block = lax.broadcasted_iota(jnp.int32, (LANES, DH), 0) // QROWS
        out[rows, :] = jnp.where(block == i, product, out[rows, :])
        new = jnp.where(total > 0.0, m + jnp.log(safe), -1e30)
        lse[pl.ds(g, 1), :] = jnp.where(team_row == i, new, lse[pl.ds(g, 1), :])

    def wide_body(r, carry):
        pl.when(count[r] > NARROW)(lambda: wide(r))
        return carry

    lax.fori_loop(0, ROWS, wide_body, 0)


SCORES = pltpu.VMEM((WIDE_CHUNKS, WIDE * PAGE, LANES), jnp.float32)
RESULT = pltpu.VMEM((ROWS * QROWS, DH), jnp.float32)


def blank_page():
    return jnp.zeros((2, PAGE, DH), jnp.bfloat16)


def attend_local_kernel(idx, count, tokens, q, pool_k, pool_v, fresh, out, lse, kv, scores, sem):
    copies = [
        pltpu.make_async_copy(pool_k, kv.at[pl.ds(1, POOL), 0], sem),
        pltpu.make_async_copy(pool_v, kv.at[pl.ds(1, POOL), 1], sem),
        pltpu.make_async_copy(fresh, kv.at[pl.ds(1 + POOL, ROWS)], sem),
    ]
    for copy in copies:
        copy.start()
    kv[0] = blank_page()
    for copy in copies:
        copy.wait()
    attention(True, idx, count, tokens, q, kv, out, lse, scores)


def attend_local(lists, q, pool_k, pool_v, fresh):
    return pl.pallas_call(
        attend_local_kernel,
        out_shape=(
            jax.ShapeDtypeStruct((ROWS * QROWS, DH), jnp.float32),
            jax.ShapeDtypeStruct((TEAMS, LANES), jnp.float32),
        ),
        in_specs=[SMEM, SMEM, SMEM, VMEM, ANY, ANY, ANY],
        out_specs=(VMEM, VMEM),
        scratch_shapes=[
            pltpu.VMEM((1 + POOL + ROWS, 2, PAGE, DH), jnp.bfloat16),
            SCORES,
            pltpu.SemaphoreType.DMA,
        ],
        compiler_params=PARAMS,
        cost_estimate=pl.CostEstimate(flops=10**9, bytes_accessed=10**7, transcendentals=10**6),
        name="attend_local",
    )(*lists, q, pool_k, pool_v, fresh)


def attend_far_kernel(idx, count, tokens, q, recv, out, lse, kv, result, scores, sem):
    copy = pltpu.make_async_copy(recv, kv.at[pl.ds(1, RECV)], sem)
    copy.start()
    kv[0] = blank_page()
    copy.wait()
    attention(False, idx, count, tokens, q, kv, result, lse, scores)
    out[...] = result[...].astype(jnp.bfloat16)


def attend_far(lists, q, recv):
    return pl.pallas_call(
        attend_far_kernel,
        out_shape=(
            jax.ShapeDtypeStruct((ROWS * QROWS, DH), jnp.bfloat16),
            jax.ShapeDtypeStruct((TEAMS, LANES), jnp.float32),
        ),
        in_specs=[SMEM, SMEM, SMEM, VMEM, ANY],
        out_specs=(VMEM, VMEM),
        scratch_shapes=[
            pltpu.VMEM((1 + RECV, 2, PAGE, DH), jnp.bfloat16),
            RESULT,
            SCORES,
            pltpu.SemaphoreType.DMA,
        ],
        compiler_params=PARAMS,
        cost_estimate=pl.CostEstimate(flops=10**9, bytes_accessed=10**7, transcendentals=10**6),
        name="attend_far",
    )(*lists, q, recv)


def finish_kernel(
    idx, count, tokens, q, recv, o1, lse1, o2, lse2, weight, out,
    kv, lse3, result, scores, heads, w, terms, sem, w_sems, out_sems,
):
    copy = pltpu.make_async_copy(recv, kv.at[pl.ds(1, RECV)], sem)
    copy.start()
    tiles, _, block = terms.shape
    loads = [
        pltpu.make_async_copy(weight.at[:, pl.ds(n * block, block)], w.at[n], w_sems.at[n]) for n in range(tiles)
    ]
    for load in loads:
        load.start()
    kv[0] = blank_page()
    copy.wait()
    attention(False, idx, count, tokens, q, kv, result, lse3, scores)

    top = jnp.maximum(jnp.maximum(lse1[...], lse2[...]), lse3[...])
    parts = [jnp.exp(x[...] - top) for x in (lse1, lse2, lse3)]
    inverse = 1.0 / (parts[0] + parts[1] + parts[2])
    f1, f2, f3 = [(x * inverse).T for x in parts]
    for g in range(TEAMS):
        rows = pl.ds(g * LANES, LANES)
        merged = f1[:, g : g + 1] * o1[rows, :] + f2[:, g : g + 1] * o2[rows, :].astype(jnp.float32)
        result[rows, :] = merged + f3[:, g : g + 1] * result[rows, :]
    for j in range(QROWS):
        t, h = j // GROUPS, j % GROUPS
        column = result[pl.ds(j, ROWS, stride=QROWS), :]
        heads[pl.ds(t * ROWS, ROWS), pl.ds(h * DH, DH)] = column.astype(jnp.bfloat16)

    stores = [pltpu.make_async_copy(terms.at[n], out.at[n], out_sems.at[n]) for n in range(tiles)]
    for n in range(tiles):
        loads[n].wait()
        terms[n] = jnp.dot(heads[...], w[n], preferred_element_type=jnp.float32).astype(jnp.bfloat16)
        stores[n].start()
    for store in stores:
        store.wait()


def finish(lists, q, recv, o1, lse1, o2, lse2, weight):
    depth, width = weight.shape
    tiles = 8
    block = width // tiles
    return pl.pallas_call(
        finish_kernel,
        out_shape=jax.ShapeDtypeStruct((tiles, STEPS * ROWS, block), jnp.bfloat16),
        in_specs=[SMEM, SMEM, SMEM, VMEM, ANY, VMEM, VMEM, VMEM, VMEM, ANY],
        out_specs=ANY,
        scratch_shapes=[
            pltpu.VMEM((1 + RECV, 2, PAGE, DH), jnp.bfloat16),
            pltpu.VMEM((TEAMS, LANES), jnp.float32),
            RESULT,
            SCORES,
            pltpu.VMEM((STEPS * ROWS, depth), jnp.bfloat16),
            pltpu.VMEM((tiles, depth, block), jnp.bfloat16),
            pltpu.VMEM((tiles, STEPS * ROWS, block), jnp.bfloat16),
            pltpu.SemaphoreType.DMA,
            pltpu.SemaphoreType.DMA((tiles,)),
            pltpu.SemaphoreType.DMA((tiles,)),
        ],
        compiler_params=PARAMS,
        name="attend_merge_project",
    )(*lists, q, recv, o1, lse1, o2, lse2, weight)


def page_lists(here, place, lengths, fresh=None):
    column = jnp.arange(MAXP, dtype=jnp.int32)[None, :]
    here = here & (column * PAGE < lengths[:, None])
    kept = here.astype(jnp.int32)
    rank = jnp.cumsum(kept, axis=1) - 1
    slot = jnp.arange(MAXP, dtype=jnp.int32)[None, :, None]
    chosen = here[:, None, :] & (rank[:, None, :] == slot)
    idx = jnp.sum(jnp.where(chosen, place[:, None, :], 0), axis=2)
    count = jnp.sum(kept, axis=1)
    tokens = jnp.sum(kept * jnp.minimum(PAGE, lengths[:, None] - column * PAGE), axis=1)
    if fresh is not None:
        idx = jnp.concatenate([fresh, idx], axis=1)
        count, tokens = count + 1, tokens + PAGE
    idx = jnp.pad(idx, ((0, 0), (0, POSITIONS - idx.shape[1])))
    return idx.reshape(-1), count, tokens


def local_lists(table, lengths):
    fresh = 1 + POOL + jnp.arange(ROWS, dtype=jnp.int32)[:, None]
    return page_lists(table < POOL, 1 + table, lengths, fresh)


def arrived_lists(table, lengths, half):
    prompt = table < POOL + N_INST * PCAP
    px, mx = table - POOL, table - (POOL + N_INST * PCAP)
    source = jnp.where(prompt, px // PCAP, mx // MCAP)
    rank = jnp.where(prompt, px % PCAP, PCAP + mx % MCAP)
    group = (source >> 3) * 4 + (source & 3)
    here = (table >= POOL) & (((source >> 2) & 1) == half)
    return page_lists(here, 1 + group * SLOTS + rank, lengths)


def by_team(queries):
    return queries.transpose(1, 0, 2, 3).reshape(TEAMS, LANES, DH)


def per_device(
    queries,
    new_keys,
    new_values,
    pool_keys,
    pool_values,
    prompt_keys,
    prompt_values,
    moved_keys,
    moved_values,
    prompt_dest,
    moved_dest,
    block_table,
    context_len,
    out_weight,
):
    page = lambda x: x.reshape(x.shape[0], PAGE, DH)
    swap = [(0, 1), (1, 0)]
    half = lax.axis_index("izh")

    def exchange(send):
        send = send.reshape(N_HALF, SLOTS, 2, PAGE, DH)
        recv = lax.all_to_all(send, HALF, split_axis=0, concat_axis=0, tiled=True)
        return recv.reshape(RECV, 2, PAGE, DH)

    far_q = lax.ppermute(queries, "izh", swap)
    far_send, near_send = pack(
        half[None], prompt_dest, moved_dest,
        page(prompt_keys), page(prompt_values), page(moved_keys), page(moved_values),
    )
    far_recv = exchange(far_send)
    near_recv = exchange(near_send)

    tables = jnp.concatenate([block_table, context_len[:, None]], axis=1)
    far_tables = lax.ppermute(tables, "izh", swap)
    fresh = jnp.stack([new_keys, new_values], axis=0).reshape(2, STEPS, ROWS, DH).transpose(2, 0, 1, 3)
    fresh = jnp.pad(fresh, ((0, 0), (0, 0), (0, PAGE - STEPS), (0, 0)))
    q = by_team(queries)
    o1, lse1 = attend_local(local_lists(block_table, context_len), q, page(pool_keys), page(pool_values), fresh)

    far_lists = arrived_lists(far_tables[:, :MAXP], far_tables[:, MAXP], half)
    o2, lse2 = attend_far(far_lists, by_team(far_q), far_recv)
    o2 = lax.ppermute(o2, "izh", swap)
    lse2 = lax.ppermute(lse2, "izh", swap)

    near_lists = arrived_lists(block_table, context_len, half)
    terms = finish(near_lists, q, near_recv, o1, lse1, o2, lse2, out_weight)
    terms = terms.reshape(4, 2, STEPS * ROWS, -1)
    got = lax.all_to_all(terms, "ty", split_axis=0, concat_axis=0, tiled=True)
    column = got.astype(jnp.float32).sum(axis=0)
    side = lax.axis_index("tz")
    mine = jnp.where(side == 0, column[0], column[1])
    other = jnp.where(side == 0, column[1], column[0]).astype(jnp.bfloat16)
    other = lax.ppermute(other, "tz", swap)
    mixed = (mine + other.astype(jnp.float32)).astype(jnp.bfloat16)
    return mixed.reshape(STEPS, ROWS, -1)


def solution(mesh):
    fine = Mesh(mesh.devices.reshape(SIZES), NAMES)
    in_specs = (
        P(None, INST, TP, None),
        P(None, INST, TP, None),
        P(None, INST, TP, None),
        P(INST, TP, None, None),
        P(INST, TP, None, None),
        P(INST, TP, None, None),
        P(INST, TP, None, None),
        P(INST, TP, None, None),
        P(INST, TP, None, None),
        P(INST),
        P(INST),
        P(INST, None),
        P(INST),
        P(TP, None),
    )
    return jax.shard_map(
        per_device, mesh=fine, in_specs=in_specs, out_specs=P(None, INST, TP), check_vma=False
    )
```

```python
import functools

import jax
import jax.numpy as jnp
from jax import lax
from jax.experimental import pallas as pl
from jax.experimental.pallas import tpu as pltpu
from jax.sharding import Mesh, PartitionSpec as P

NAMES = ("ix", "izh", "izl", "ic", "ty", "tz")
SIZES = (4, 2, 2, 2, 4, 2)
INST = ("ix", "izh", "izl", "ic")
HALF = ("ix", "izl", "ic")
TP = ("ty", "tz")

N_INST = 32
N_HALF = 16
STEPS, ROWS, GROUPS, DH = 4, 64, 8, 128
QROWS = STEPS * GROUPS
PAGE, MAXP = 16, 48
POOL, OUT, MIG = 192, 192, 96
PCAP, MCAP = 12, 6
SLOTS = PCAP + MCAP
RECV = N_HALF * SLOTS
NARROW = 8
WIDE = 16
WIDE_CHUNKS = 4
UNROLL = 2
POSITIONS = WIDE * WIDE_CHUNKS
TEAM = 4
TEAMS = ROWS // TEAM
LANES = TEAM * QROWS
SCALE = DH ** -0.5
VMEM_LIMIT = 63 * 1024 * 1024

SMEM = pl.BlockSpec(memory_space=pltpu.SMEM)
VMEM = pl.BlockSpec(memory_space=pltpu.VMEM)
ANY = pl.BlockSpec(memory_space=pl.ANY)
PARAMS = pltpu.CompilerParams(vmem_limit_bytes=VMEM_LIMIT)


def pack_kernel(half, pdest, mdest, pk, pv, mk, mv, *refs):
    out, pages, send, count, sems, out_sem = refs[-6:]
    loads = [
        pltpu.make_async_copy(pk, pages.at[pl.ds(0, OUT), 0], sems.at[0]),
        pltpu.make_async_copy(pv, pages.at[pl.ds(0, OUT), 1], sems.at[1]),
        pltpu.make_async_copy(mk, pages.at[pl.ds(OUT, MIG), 0], sems.at[2]),
        pltpu.make_async_copy(mv, pages.at[pl.ds(OUT, MIG), 1], sems.at[3]),
    ]
    for load in loads:
        load.start()
    wanted = half[0]

    def clear(i, carry):
        count[i] = 0
        return carry

    def place(dest, first, origin, j):
        d = dest[j]
        k = count[d]
        count[d] = k + 1
        group = (d >> 3) * 4 + (d & 3)
        slot = jnp.where(((d >> 2) & 1) == wanted, group * SLOTS + first + k, RECV)
        send[slot] = pages[origin + j]

    def prompt(j, carry):
        place(pdest, 0, 0, j)
        return carry

    def moved(j, carry):
        place(mdest, PCAP, OUT, j)
        return carry

    lax.fori_loop(0, N_INST, clear, 0)
    loads[0].wait()
    loads[1].wait()
    lax.fori_loop(0, OUT, prompt, 0, unroll=4)
    lax.fori_loop(0, N_INST, clear, 0)
    loads[2].wait()
    loads[3].wait()
    lax.fori_loop(0, MIG, moved, 0, unroll=4)
    store = pltpu.make_async_copy(send.at[pl.ds(0, RECV)], out, out_sem)
    store.start()
    store.wait()


def pack(half, pdest, mdest, pk, pv, mk, mv, *after):
    return pl.pallas_call(
        pack_kernel,
        out_shape=jax.ShapeDtypeStruct((RECV, 2, PAGE, DH), jnp.bfloat16),
        in_specs=[SMEM, SMEM, SMEM] + [ANY] * (4 + len(after)),
        out_specs=ANY,
        scratch_shapes=[
            pltpu.VMEM((OUT + MIG, 2, PAGE, DH), jnp.bfloat16),
            pltpu.VMEM((RECV + 1, 2, PAGE, DH), jnp.bfloat16),
            pltpu.SMEM((N_INST,), jnp.int32),
            pltpu.SemaphoreType.DMA((4,)),
            pltpu.SemaphoreType.DMA,
        ],
        compiler_params=PARAMS,
        cost_estimate=pl.CostEstimate(flops=10**6, bytes_accessed=10**7, transcendentals=0),
        name="pack_pages",
    )(half, pdest, mdest, pk, pv, mk, mv, *after)


def gate_kernel(x, *refs):
    pass


def gate(x, *after):
    return pl.pallas_call(
        gate_kernel,
        out_shape=jax.ShapeDtypeStruct(x.shape, x.dtype),
        in_specs=[ANY] * (1 + len(after)),
        out_specs=ANY,
        input_output_aliases={0: 0},
        name="gate",
    )(x, *after)


def attention(fresh, lists, q, kv, out, lse, scores):
    lane = lax.broadcasted_iota(jnp.int32, (1, LANES), 1)
    team_row = lane // QROWS
    step = (lane % QROWS) // GROUPS

    def load(r, first, n, which):
        return [kv[lists[r * POSITIONS + first + p], which] for p in range(n)]

    def count(r):
        return lists[ROWS * POSITIONS + r]

    def tokens(r):
        return lists[ROWS * POSITIONS + ROWS + r]

    def mask(s, first, limit):
        token = lax.broadcasted_iota(jnp.int32, s.shape, 0) + first
        seen = token < limit
        if fresh:
            seen = token < jnp.where(token < PAGE, step + 1, limit)
        return jnp.where(seen, s * SCALE, -jnp.inf)

    def dot_nt(a, b):
        return lax.dot_general(a, b, (((1,), (1,)), ((), ())), preferred_element_type=jnp.float32)

    def narrow(g):
        width = NARROW * PAGE
        rows = [g * TEAM + i for i in range(TEAM)]
        keys = jnp.concatenate([k for r in rows for k in load(r, 0, NARROW, 0)], axis=0)
        s_all = dot_nt(keys, q[g])
        s = s_all[:width]
        limit = jnp.full((1, LANES), tokens(rows[0]), jnp.int32)
        owner = lax.broadcasted_iota(jnp.int32, (width, LANES), 1) // QROWS
        for i in range(1, TEAM):
            s = jnp.where(owner == i, s_all[i * width : (i + 1) * width], s)
            limit = jnp.where(team_row == i, tokens(rows[i]), limit)
        s = mask(s, 0, limit)
        m = jnp.maximum(jnp.max(s, axis=0, keepdims=True), -1e30)
        e = jnp.exp(s - m)
        total = jnp.sum(e, axis=0, keepdims=True)
        safe = jnp.maximum(total, 1e-30)
        lse[pl.ds(g, 1), :] = jnp.where(total > 0.0, m + jnp.log(safe), -1e30)
        weights = (e * (1.0 / safe)).T.astype(jnp.bfloat16)
        for i in range(TEAM):
            values = jnp.concatenate(load(rows[i], 0, NARROW, 1), axis=0)
            part = weights[i * QROWS : (i + 1) * QROWS]
            first = pl.multiple_of(g * LANES + i * QROWS, QROWS)
            out[pl.ds(first, QROWS), :] = jnp.dot(part, values, preferred_element_type=jnp.float32)

    def narrow_body(n, carry):
        for u in range(UNROLL):
            narrow(n * UNROLL + u)
        return carry

    lax.fori_loop(0, TEAMS // UNROLL, narrow_body, 0)

    def wide(r):
        width = WIDE * PAGE
        chunks = (count(r) + WIDE - 1) // WIDE
        g, i = r // TEAM, r % TEAM

        def first_pass(c, m):
            keys = jnp.concatenate(load(r, c * WIDE, WIDE, 0), axis=0)
            s = mask(dot_nt(keys, q[g]), c * width, tokens(r))
            scores[c] = s
            return jnp.maximum(m, jnp.max(s, axis=0, keepdims=True))

        m = lax.fori_loop(0, chunks, first_pass, jnp.full((1, LANES), -1e30, jnp.float32))

        def second_pass(c, total):
            e = jnp.exp(scores[c] - m)
            scores[c] = e
            return total + jnp.sum(e, axis=0, keepdims=True)

        total = lax.fori_loop(0, chunks, second_pass, jnp.zeros((1, LANES), jnp.float32))
        safe = jnp.maximum(total, 1e-30)
        inverse = 1.0 / safe

        def third_pass(c, product):
            weights = (scores[c] * inverse).T.astype(jnp.bfloat16)
            values = jnp.concatenate(load(r, c * WIDE, WIDE, 1), axis=0)
            return product + jnp.dot(weights, values, preferred_element_type=jnp.float32)

        product = lax.fori_loop(0, chunks, third_pass, jnp.zeros((LANES, DH), jnp.float32))
        rows = pl.ds(pl.multiple_of(g * LANES, LANES), LANES)
        block = lax.broadcasted_iota(jnp.int32, (LANES, DH), 0) // QROWS
        out[rows, :] = jnp.where(block == i, product, out[rows, :])
        new = jnp.where(total > 0.0, m + jnp.log(safe), -1e30)
        lse[pl.ds(g, 1), :] = jnp.where(team_row == i, new, lse[pl.ds(g, 1), :])

    def wide_body(r, carry):
        pl.when(count(r) > NARROW)(lambda: wide(r))
        return carry

    lax.fori_loop(0, ROWS, wide_body, 0)


SCORES = pltpu.VMEM((WIDE_CHUNKS, WIDE * PAGE, LANES), jnp.float32)
RESULT = pltpu.VMEM((ROWS * QROWS, DH), jnp.float32)


def blank_page():
    return jnp.zeros((2, PAGE, DH), jnp.bfloat16)


def attend_local_kernel(lists, q, pool_k, pool_v, fresh, out, lse, kv, scores, sem):
    copies = [
        pltpu.make_async_copy(pool_k, kv.at[pl.ds(1, POOL), 0], sem),
        pltpu.make_async_copy(pool_v, kv.at[pl.ds(1, POOL), 1], sem),
        pltpu.make_async_copy(fresh, kv.at[pl.ds(1 + POOL, ROWS)], sem),
    ]
    for copy in copies:
        copy.start()
    kv[0] = blank_page()
    for copy in copies:
        copy.wait()
    attention(True, lists, q, kv, out, lse, scores)


def attend_local(lists, q, pool_k, pool_v, fresh):
    return pl.pallas_call(
        attend_local_kernel,
        out_shape=(
            jax.ShapeDtypeStruct((ROWS * QROWS, DH), jnp.float32),
            jax.ShapeDtypeStruct((TEAMS, LANES), jnp.float32),
        ),
        in_specs=[SMEM, VMEM, ANY, ANY, ANY],
        out_specs=(VMEM, VMEM),
        scratch_shapes=[
            pltpu.VMEM((1 + POOL + ROWS, 2, PAGE, DH), jnp.bfloat16),
            SCORES,
            pltpu.SemaphoreType.DMA,
        ],
        compiler_params=PARAMS,
        cost_estimate=pl.CostEstimate(flops=10**9, bytes_accessed=10**7, transcendentals=10**6),
        name="attend_local",
    )(lists, q, pool_k, pool_v, fresh)


def attend_far_kernel(lists, q, recv, out, lse, kv, result, scores, sem):
    copy = pltpu.make_async_copy(recv, kv.at[pl.ds(1, RECV)], sem)
    copy.start()
    kv[0] = blank_page()
    copy.wait()
    attention(False, lists, q, kv, result, lse, scores)
    out[...] = result[...].astype(jnp.bfloat16)


def attend_far(lists, q, recv):
    return pl.pallas_call(
        attend_far_kernel,
        out_shape=(
            jax.ShapeDtypeStruct((ROWS * QROWS, DH), jnp.bfloat16),
            jax.ShapeDtypeStruct((TEAMS, LANES), jnp.float32),
        ),
        in_specs=[SMEM, VMEM, ANY],
        out_specs=(VMEM, VMEM),
        scratch_shapes=[
            pltpu.VMEM((1 + RECV, 2, PAGE, DH), jnp.bfloat16),
            RESULT,
            SCORES,
            pltpu.SemaphoreType.DMA,
        ],
        compiler_params=PARAMS,
        cost_estimate=pl.CostEstimate(flops=10**9, bytes_accessed=10**7, transcendentals=10**6),
        name="attend_far",
    )(lists, q, recv)


SHIFTS = (2, 1, 3, 0)
BLOCK = 512


def column_tile(place, side, shift, weight):
    y = lax.rem(place[0] + shift, 4)
    z = place[1] if side == 0 else 1 - place[1]
    return weight.at[:, pl.ds(pl.multiple_of((y * 2 + z) * BLOCK, BLOCK), BLOCK)]


def start_tiles(place, side, weight, w, w_sems):
    loads = [
        pltpu.make_async_copy(column_tile(place, side, shift, weight), w.at[n], w_sems.at[n])
        for n, shift in enumerate(SHIFTS)
    ]
    for load in loads:
        load.start()
    return loads


def project(loads, heads, w, outs, terms, out_sems):
    stores = []
    for n, load in enumerate(loads):
        load.wait()
        terms[n] = jnp.dot(heads[...], w[n], preferred_element_type=jnp.float32).astype(jnp.bfloat16)
        store = pltpu.make_async_copy(terms.at[n], outs[n], out_sems.at[n])
        store.start()
        stores.append(store)
    for store in stores:
        store.wait()


TILES = len(SHIFTS)
TERMS = (jax.ShapeDtypeStruct((STEPS * ROWS, BLOCK), jnp.bfloat16),) * TILES
PROJECT_SCRATCH = [
    pltpu.VMEM((TILES, GROUPS * DH, BLOCK), jnp.bfloat16),
    pltpu.VMEM((TILES, STEPS * ROWS, BLOCK), jnp.bfloat16),
    pltpu.SemaphoreType.DMA((TILES,)),
    pltpu.SemaphoreType.DMA((TILES,)),
]


def finish_kernel(place, lists, q, recv, o1, lse1, o2, lse2, weight, heads, *refs):
    outs, (kv, lse3, result, scores, sem, w, terms, w_sems, out_sems) = refs[:TILES], refs[TILES:]
    copy = pltpu.make_async_copy(recv, kv.at[pl.ds(1, RECV)], sem)
    copy.start()
    loads = start_tiles(place, 1, weight, w, w_sems)
    kv[0] = blank_page()
    copy.wait()
    attention(False, lists, q, kv, result, lse3, scores)

    top = jnp.maximum(jnp.maximum(lse1[...], lse2[...]), lse3[...])
    parts = [jnp.exp(x[...] - top) for x in (lse1, lse2, lse3)]
    inverse = 1.0 / (parts[0] + parts[1] + parts[2])
    f1, f2, f3 = [(x * inverse).T for x in parts]
    for g in range(TEAMS):
        rows = pl.ds(g * LANES, LANES)
        merged = f1[:, g : g + 1] * o1[rows, :] + f2[:, g : g + 1] * o2[rows, :].astype(jnp.float32)
        result[rows, :] = merged + f3[:, g : g + 1] * result[rows, :]
    for j in range(QROWS):
        t, h = j // GROUPS, j % GROUPS
        column = result[pl.ds(j, ROWS, stride=QROWS), :]
        heads[pl.ds(t * ROWS, ROWS), pl.ds(h * DH, DH)] = column.astype(jnp.bfloat16)
    project(loads, heads, w, outs, terms, out_sems)


def finish(place, lists, q, recv, o1, lse1, o2, lse2, weight):
    heads = jax.ShapeDtypeStruct((STEPS * ROWS, GROUPS * DH), jnp.bfloat16)
    heads, *terms = pl.pallas_call(
        finish_kernel,
        out_shape=(heads,) + TERMS,
        in_specs=[SMEM, SMEM, VMEM, ANY, VMEM, VMEM, VMEM, VMEM, ANY],
        out_specs=(VMEM,) + (ANY,) * TILES,
        scratch_shapes=[
            pltpu.VMEM((1 + RECV, 2, PAGE, DH), jnp.bfloat16),
            pltpu.VMEM((TEAMS, LANES), jnp.float32),
            RESULT,
            SCORES,
            pltpu.SemaphoreType.DMA,
        ] + PROJECT_SCRATCH,
        compiler_params=PARAMS,
        name="attend_merge_project",
    )(place, lists, q, recv, o1, lse1, o2, lse2, weight)
    return heads, terms


def project_kernel(place, heads, weight, *refs):
    outs, (w, terms, w_sems, out_sems) = refs[:TILES], refs[TILES:]
    project(start_tiles(place, 0, weight, w, w_sems), heads, w, outs, terms, out_sems)


def project_mine(place, heads, weight):
    return pl.pallas_call(
        project_kernel,
        out_shape=TERMS,
        in_specs=[SMEM, VMEM, ANY],
        out_specs=(ANY,) * TILES,
        scratch_shapes=PROJECT_SCRATCH,
        compiler_params=PARAMS,
        cost_estimate=pl.CostEstimate(flops=10**9, bytes_accessed=6 * 10**6, transcendentals=0),
        name="project_mine",
    )(place, heads, weight)


def sum_over_y(terms):
    total = terms[SHIFTS.index(0)].astype(jnp.float32)
    for term, shift in zip(terms, SHIFTS):
        if shift:
            moved = lax.ppermute(term, "ty", [(i, (i + shift) % 4) for i in range(4)])
            total = total + moved.astype(jnp.float32)
    return total


def page_lists(here, place, lengths, fresh=None):
    column = jnp.arange(MAXP, dtype=jnp.int32)[None, :]
    here = here & (column * PAGE < lengths[:, None])
    kept = here.astype(jnp.int32)
    rank = jnp.cumsum(kept, axis=1) - 1
    slot = jnp.arange(MAXP, dtype=jnp.int32)[None, :, None]
    chosen = here[:, None, :] & (rank[:, None, :] == slot)
    idx = jnp.sum(jnp.where(chosen, place[:, None, :], 0), axis=2)
    count = jnp.sum(kept, axis=1)
    tokens = jnp.sum(kept * jnp.minimum(PAGE, lengths[:, None] - column * PAGE), axis=1)
    if fresh is not None:
        idx = jnp.concatenate([fresh, idx], axis=1)
        count, tokens = count + 1, tokens + PAGE
    idx = jnp.pad(idx, ((0, 0), (0, POSITIONS - idx.shape[1])))
    return jnp.concatenate([idx.reshape(-1), count, tokens])


def local_lists(table, lengths):
    fresh = 1 + POOL + jnp.arange(ROWS, dtype=jnp.int32)[:, None]
    return page_lists(table < POOL, 1 + table, lengths, fresh)


def arrived_lists(table, lengths, half):
    prompt = table < POOL + N_INST * PCAP
    px, mx = table - POOL, table - (POOL + N_INST * PCAP)
    source = jnp.where(prompt, px // PCAP, mx // MCAP)
    rank = jnp.where(prompt, px % PCAP, PCAP + mx % MCAP)
    group = (source >> 3) * 4 + (source & 3)
    here = (table >= POOL) & (((source >> 2) & 1) == half)
    return page_lists(here, 1 + group * SLOTS + rank, lengths)


def by_team(queries):
    return queries.transpose(1, 0, 2, 3).reshape(TEAMS, LANES, DH)


def per_device(
    queries,
    new_keys,
    new_values,
    pool_keys,
    pool_values,
    prompt_keys,
    prompt_values,
    moved_keys,
    moved_values,
    prompt_dest,
    moved_dest,
    block_table,
    context_len,
    out_weight,
):
    page = lambda x: x.reshape(x.shape[0], PAGE, DH)
    swap = [(0, 1), (1, 0)]
    half = lax.axis_index("izh")

    def exchange(send):
        send = send.reshape(N_HALF, SLOTS, 2, PAGE, DH)
        recv = lax.all_to_all(send, HALF, split_axis=0, concat_axis=0, tiled=True)
        return recv.reshape(RECV, 2, PAGE, DH)

    pages = (page(prompt_keys), page(prompt_values), page(moved_keys), page(moved_values))
    far_recv = exchange(pack((1 - half)[None], prompt_dest, moved_dest, *pages))
    far_q = by_team(lax.ppermute(queries, "izh", swap))
    far_lists = lax.ppermute(arrived_lists(block_table, context_len, 1 - half), "izh", swap)
    near_lists = arrived_lists(block_table, context_len, half)

    fresh = jnp.stack([new_keys, new_values], axis=0).reshape(2, STEPS, ROWS, DH).transpose(2, 0, 1, 3)
    fresh = jnp.pad(fresh, ((0, 0), (0, 0), (0, PAGE - STEPS), (0, 0)))
    q = by_team(queries)
    o1, lse1 = attend_local(local_lists(block_table, context_len), q, page(pool_keys), page(pool_values), fresh)
    near_send = pack(half[None], prompt_dest, moved_dest, *pages, lse1)
    near_recv = exchange(gate(near_send, far_q, far_lists, near_lists))

    o2, lse2 = attend_far(far_lists, far_q, far_recv)
    o2 = lax.ppermute(o2, "izh", swap)
    lse2 = lax.ppermute(lse2, "izh", swap)

    place = jnp.stack([lax.axis_index("ty"), lax.axis_index("tz")]).astype(jnp.int32)
    heads, terms = finish(place, near_lists, q, near_recv, o1, lse1, o2, lse2, out_weight)
    other = lax.ppermute(sum_over_y(terms).astype(jnp.bfloat16), "tz", swap)
    mine = sum_over_y(project_mine(place, heads, out_weight))
    return (mine + other.astype(jnp.float32)).astype(jnp.bfloat16).reshape(STEPS, ROWS, -1)


def solution(mesh):
    fine = Mesh(mesh.devices.reshape(SIZES), NAMES)
    in_specs = (
        P(None, INST, TP, None),
        P(None, INST, TP, None),
        P(None, INST, TP, None),
        P(INST, TP, None, None),
        P(INST, TP, None, None),
        P(INST, TP, None, None),
        P(INST, TP, None, None),
        P(INST, TP, None, None),
        P(INST, TP, None, None),
        P(INST),
        P(INST),
        P(INST, None),
        P(INST),
        P(TP, None),
    )
    return jax.shard_map(
        per_device, mesh=fine, in_specs=in_specs, out_specs=P(None, INST, TP), check_vma=False
    )
```

```python
import functools

import jax
import jax.numpy as jnp
from jax import lax
from jax.experimental import pallas as pl
from jax.experimental.pallas import tpu as pltpu
from jax.sharding import Mesh, PartitionSpec as P

NAMES = ("ix", "izh", "izl", "ic", "ty", "tz")
SIZES = (4, 2, 2, 2, 4, 2)
INST = ("ix", "izh", "izl", "ic")
HALF = ("ix", "izl", "ic")
TP = ("ty", "tz")

N_INST = 32
N_HALF = 16
STEPS, ROWS, GROUPS, DH = 4, 64, 8, 128
QROWS = STEPS * GROUPS
PAGE, MAXP = 16, 48
POOL, OUT, MIG = 192, 192, 96
PCAP, MCAP = 12, 6
SLOTS = PCAP + MCAP
RECV = N_HALF * SLOTS
NARROW = 8
WIDE = 16
WIDE_CHUNKS = 4
POSITIONS = WIDE * WIDE_CHUNKS
LIST = ROWS * (POSITIONS + 2)
TEAM = 4
TEAMS = ROWS // TEAM
LANES = TEAM * QROWS
SCALE = DH ** -0.5
VMEM_LIMIT = 63 * 1024 * 1024

SMEM = pl.BlockSpec(memory_space=pltpu.SMEM)
VMEM = pl.BlockSpec(memory_space=pltpu.VMEM)
ANY = pl.BlockSpec(memory_space=pl.ANY)
PARAMS = pltpu.CompilerParams(vmem_limit_bytes=VMEM_LIMIT)


def start_all(pairs, sems):
    copies = [pltpu.make_async_copy(src, dst, sems.at[n]) for n, (src, dst) in enumerate(pairs)]
    for copy in copies:
        copy.start()
    return copies


def wait_all(copies):
    for copy in copies:
        copy.wait()


def pack_kernel(half, pdest, mdest, pk, pv, mk, mv, *refs):
    out, pages, send, pdest_s, mdest_s, slots, count, sems, out_sem = refs[-9:]
    loads = start_all(
        [
            (pdest, pdest_s),
            (mdest, mdest_s),
            (pk, pages.at[pl.ds(0, OUT), 0]),
            (pv, pages.at[pl.ds(0, OUT), 1]),
            (mk, pages.at[pl.ds(OUT, MIG), 0]),
            (mv, pages.at[pl.ds(OUT, MIG), 1]),
        ],
        sems,
    )
    wanted = half[0]
    for d in range(N_INST):
        count[d] = 0
        count[N_INST + d] = PCAP
    wait_all(loads[:2])

    def rank(dest, kind, first, j, carry):
        d = dest[j]
        k = count[kind + d]
        count[kind + d] = k + 1
        group = (d >> 3) * 4 + (d & 3)
        slots[first + j] = jnp.where(((d >> 2) & 1) == wanted, group * SLOTS + k, RECV)
        return carry

    def copy_page(j, carry):
        send[slots[j]] = pages[j]
        return carry

    lax.fori_loop(0, OUT, functools.partial(rank, pdest_s, 0, 0), 0, unroll=8)
    lax.fori_loop(0, MIG, functools.partial(rank, mdest_s, N_INST, OUT), 0, unroll=8)
    wait_all(loads[2:])
    lax.fori_loop(0, OUT + MIG, copy_page, 0, unroll=8)
    wait_all(start_all([(send.at[pl.ds(0, RECV)], out)], out_sem))


def pack(half, pdest, mdest, pk, pv, mk, mv, *after):
    return pl.pallas_call(
        pack_kernel,
        out_shape=jax.ShapeDtypeStruct((RECV, 2, PAGE, DH), jnp.bfloat16),
        in_specs=[SMEM] + [ANY] * (6 + len(after)),
        out_specs=ANY,
        scratch_shapes=[
            pltpu.VMEM((OUT + MIG, 2, PAGE, DH), jnp.bfloat16),
            pltpu.VMEM((RECV + 1, 2, PAGE, DH), jnp.bfloat16),
            pltpu.SMEM((OUT,), jnp.int32),
            pltpu.SMEM((MIG,), jnp.int32),
            pltpu.SMEM((OUT + MIG,), jnp.int32),
            pltpu.SMEM((2 * N_INST,), jnp.int32),
            pltpu.SemaphoreType.DMA((6,)),
            pltpu.SemaphoreType.DMA((1,)),
        ],
        compiler_params=PARAMS,
        cost_estimate=pl.CostEstimate(flops=10**6, bytes_accessed=10**7, transcendentals=0),
        name="pack_pages",
    )(half, pdest, mdest, pk, pv, mk, mv, *after)


def gate_kernel(x, *refs):
    pass


def gate(x, *after):
    return pl.pallas_call(
        gate_kernel,
        out_shape=jax.ShapeDtypeStruct(x.shape, x.dtype),
        in_specs=[ANY] * (1 + len(after)),
        out_specs=ANY,
        input_output_aliases={0: 0},
        name="gate",
    )(x, *after)


def attention(fresh, lists, q, kv, out, lse, scores):
    lane = lax.broadcasted_iota(jnp.int32, (1, LANES), 1)
    team_row = (lane // GROUPS) % TEAM
    step = lane // (TEAM * GROUPS)

    def load(r, first, n, which):
        return [kv[lists[r * POSITIONS + first + p], which] for p in range(n)]

    def count(r):
        return lists[ROWS * POSITIONS + r]

    def tokens(r):
        return lists[ROWS * POSITIONS + ROWS + r]

    def team(t, g):
        first = t * ROWS * GROUPS + g * TEAM * GROUPS
        return pl.ds(first if isinstance(g, int) else pl.multiple_of(first, TEAM * GROUPS), TEAM * GROUPS)

    def queries(g):
        return jnp.concatenate([q[team(t, g), :] for t in range(STEPS)], axis=0)

    def mask(s, first, limit):
        token = lax.broadcasted_iota(jnp.int32, s.shape, 0) + first
        seen = token < limit
        if fresh:
            seen = token < jnp.where(token < PAGE, step + 1, limit)
        return jnp.where(seen, s * SCALE, -jnp.inf)

    def dot_nt(a, b):
        return lax.dot_general(a, b, (((1,), (1,)), ((), ())), preferred_element_type=jnp.float32)

    def narrow(g):
        width = NARROW * PAGE
        rows = [g * TEAM + i for i in range(TEAM)]
        keys = jnp.concatenate([k for r in rows for k in load(r, 0, NARROW, 0)], axis=0)
        s_all = dot_nt(keys, queries(g))
        s = s_all[:width]
        limit = jnp.full((1, LANES), tokens(rows[0]), jnp.int32)
        owner = (lax.broadcasted_iota(jnp.int32, (width, LANES), 1) // GROUPS) % TEAM
        for i in range(1, TEAM):
            s = jnp.where(owner == i, s_all[i * width : (i + 1) * width], s)
            limit = jnp.where(team_row == i, tokens(rows[i]), limit)
        s = mask(s, 0, limit)
        m = jnp.maximum(jnp.max(s, axis=0, keepdims=True), -1e30)
        e = jnp.exp(s - m)
        total = jnp.sum(e, axis=0, keepdims=True)
        safe = jnp.maximum(total, 1e-30)
        lse[pl.ds(g, 1), :] = jnp.where(total > 0.0, m + jnp.log(safe), -1e30)
        weights = (e * (1.0 / safe)).T
        for i in range(TEAM):
            values = jnp.concatenate(load(rows[i], 0, NARROW, 1), axis=0)
            pieces = [weights[(t * TEAM + i) * GROUPS : (t * TEAM + i + 1) * GROUPS] for t in range(STEPS)]
            part = jnp.concatenate(pieces, axis=0).astype(jnp.bfloat16)
            product = jnp.dot(part, values, preferred_element_type=jnp.float32)
            for t in range(STEPS):
                first = (t * ROWS + rows[i]) * GROUPS
                out[pl.ds(first, GROUPS), :] = product[t * GROUPS : (t + 1) * GROUPS]

    for g in range(TEAMS):
        narrow(g)

    def wide(r):
        width = WIDE * PAGE
        chunks = (count(r) + WIDE - 1) // WIDE
        g, i = r // TEAM, r % TEAM

        def first_pass(c, m):
            keys = jnp.concatenate(load(r, c * WIDE, WIDE, 0), axis=0)
            s = mask(dot_nt(keys, queries(g)), c * width, tokens(r))
            scores[c] = s
            return jnp.maximum(m, jnp.max(s, axis=0, keepdims=True))

        m = lax.fori_loop(0, chunks, first_pass, jnp.full((1, LANES), -1e30, jnp.float32))

        def second_pass(c, total):
            e = jnp.exp(scores[c] - m)
            scores[c] = e
            return total + jnp.sum(e, axis=0, keepdims=True)

        total = lax.fori_loop(0, chunks, second_pass, jnp.zeros((1, LANES), jnp.float32))
        safe = jnp.maximum(total, 1e-30)
        inverse = 1.0 / safe

        def third_pass(c, product):
            weights = (scores[c] * inverse).T.astype(jnp.bfloat16)
            values = jnp.concatenate(load(r, c * WIDE, WIDE, 1), axis=0)
            return product + jnp.dot(weights, values, preferred_element_type=jnp.float32)

        product = lax.fori_loop(0, chunks, third_pass, jnp.zeros((LANES, DH), jnp.float32))
        size = TEAM * GROUPS
        owner = lax.broadcasted_iota(jnp.int32, (size, DH), 0) // GROUPS
        for t in range(STEPS):
            rows = team(t, g)
            out[rows, :] = jnp.where(owner == i, product[t * size : (t + 1) * size], out[rows, :])
        new = jnp.where(total > 0.0, m + jnp.log(safe), -1e30)
        lse[pl.ds(g, 1), :] = jnp.where(team_row == i, new, lse[pl.ds(g, 1), :])

    def wide_body(r, carry):
        pl.when(count(r) > NARROW)(lambda: wide(r))
        return carry

    lax.fori_loop(0, ROWS, wide_body, 0)


QUERIES = pltpu.VMEM((ROWS * QROWS, DH), jnp.bfloat16)
SCORES = pltpu.VMEM((WIDE_CHUNKS, WIDE * PAGE, LANES), jnp.float32)
RESULT = pltpu.VMEM((ROWS * QROWS, DH), jnp.float32)
LSE = pltpu.VMEM((TEAMS, LANES), jnp.float32)
LISTS = pltpu.SMEM((LIST,), jnp.int32)


def pages_scratch(n):
    return pltpu.VMEM((1 + n, 2, PAGE, DH), jnp.bfloat16)


def blank_page():
    return jnp.zeros((2, PAGE, DH), jnp.bfloat16)


def attend_local_kernel(lists, q, pool_k, pool_v, fresh, out, lse, lists_s, q_s, kv, scores, sems):
    copies = start_all(
        [
            (lists, lists_s),
            (q, q_s),
            (pool_k, kv.at[pl.ds(1, POOL), 0]),
            (pool_v, kv.at[pl.ds(1, POOL), 1]),
            (fresh, kv.at[pl.ds(1 + POOL, ROWS)]),
        ],
        sems,
    )
    kv[0] = blank_page()
    wait_all(copies)
    attention(True, lists_s, q_s, kv, out, lse, scores)


def attend_local(lists, q, pool_k, pool_v, fresh):
    return pl.pallas_call(
        attend_local_kernel,
        out_shape=(
            jax.ShapeDtypeStruct((ROWS * QROWS, DH), jnp.float32),
            jax.ShapeDtypeStruct((TEAMS, LANES), jnp.float32),
        ),
        in_specs=[ANY] * 5,
        out_specs=(VMEM, VMEM),
        scratch_shapes=[LISTS, QUERIES, pages_scratch(POOL + ROWS), SCORES, pltpu.SemaphoreType.DMA((5,))],
        compiler_params=PARAMS,
        cost_estimate=pl.CostEstimate(flops=10**9, bytes_accessed=10**7, transcendentals=10**6),
        name="attend_local",
    )(lists, q, pool_k, pool_v, fresh)


def attend_far_kernel(lists, q, recv, out, lse, lists_s, q_s, kv, result, scores, sems):
    copies = start_all([(lists, lists_s), (q, q_s), (recv, kv.at[pl.ds(1, RECV)])], sems)
    kv[0] = blank_page()
    wait_all(copies)
    attention(False, lists_s, q_s, kv, result, lse, scores)
    out[...] = result[...].astype(jnp.bfloat16)


def attend_far(lists, q, recv):
    return pl.pallas_call(
        attend_far_kernel,
        out_shape=(
            jax.ShapeDtypeStruct((ROWS * QROWS, DH), jnp.bfloat16),
            jax.ShapeDtypeStruct((TEAMS, LANES), jnp.float32),
        ),
        in_specs=[ANY] * 3,
        out_specs=(VMEM, VMEM),
        scratch_shapes=[LISTS, QUERIES, pages_scratch(RECV), RESULT, SCORES, pltpu.SemaphoreType.DMA((3,))],
        compiler_params=PARAMS,
        cost_estimate=pl.CostEstimate(flops=10**9, bytes_accessed=10**7, transcendentals=10**6),
        name="attend_far",
    )(lists, q, recv)


SHIFTS = (2, 1, 3, 0)
BLOCK = 512


def column_tile(place, side, shift, weight):
    y = lax.rem(place[0] + shift, 4)
    z = place[1] if side == 0 else 1 - place[1]
    return weight.at[:, pl.ds(pl.multiple_of((y * 2 + z) * BLOCK, BLOCK), BLOCK)]


def start_tiles(place, side, weight, w, w_sems):
    loads = [
        pltpu.make_async_copy(column_tile(place, side, shift, weight), w.at[n], w_sems.at[n])
        for n, shift in enumerate(SHIFTS)
    ]
    for load in loads:
        load.start()
    return loads


def project(loads, heads, w, outs, terms, out_sems):
    stores = []
    for n, load in enumerate(loads):
        load.wait()
        terms[n] = jnp.dot(heads[...], w[n], preferred_element_type=jnp.float32).astype(jnp.bfloat16)
        store = pltpu.make_async_copy(terms.at[n], outs[n], out_sems.at[n])
        store.start()
        stores.append(store)
    for store in stores:
        store.wait()


TILES = len(SHIFTS)
TERMS = (jax.ShapeDtypeStruct((STEPS * ROWS, BLOCK), jnp.bfloat16),) * TILES
PROJECT_SCRATCH = [
    pltpu.VMEM((TILES, GROUPS * DH, BLOCK), jnp.bfloat16),
    pltpu.VMEM((TILES, STEPS * ROWS, BLOCK), jnp.bfloat16),
    pltpu.SemaphoreType.DMA((TILES,)),
    pltpu.SemaphoreType.DMA((TILES,)),
]


def finish_kernel(place, lists, q, recv, o1, lse1, o2, lse2, weight, heads, *refs):
    outs, refs = refs[:TILES], refs[TILES:]
    lists_s, q_s, kv, o1_s, lse1_s, o2_s, lse2_s, lse3, result, scores, sems, w, terms, w_sems, out_sems = refs
    copies = start_all(
        [
            (lists, lists_s),
            (q, q_s),
            (recv, kv.at[pl.ds(1, RECV)]),
            (lse1, lse1_s),
            (lse2, lse2_s),
            (o1, o1_s),
            (o2, o2_s),
        ],
        sems,
    )
    kv[0] = blank_page()
    wait_all(copies[:3])
    loads = start_tiles(place, 1, weight, w, w_sems)
    attention(False, lists_s, q_s, kv, result, lse3, scores)
    wait_all(copies[3:])

    top = jnp.maximum(jnp.maximum(lse1_s[...], lse2_s[...]), lse3[...])
    parts = [jnp.exp(x[...] - top) for x in (lse1_s, lse2_s, lse3)]
    inverse = 1.0 / (parts[0] + parts[1] + parts[2])
    f1, f2, f3 = [(x * inverse).T for x in parts]
    size = TEAM * GROUPS
    for t in range(STEPS):
        for g in range(TEAMS):
            rows = pl.ds((t * TEAMS + g) * size, size)
            lanes = slice(t * size, (t + 1) * size)
            merged = f1[lanes, g : g + 1] * o1_s[rows, :] + f2[lanes, g : g + 1] * o2_s[rows, :].astype(jnp.float32)
            result[rows, :] = merged + f3[lanes, g : g + 1] * result[rows, :]
        for h in range(GROUPS):
            column = result[pl.ds(t * ROWS * GROUPS + h, ROWS, stride=GROUPS), :]
            heads[pl.ds(t * ROWS, ROWS), pl.ds(h * DH, DH)] = column.astype(jnp.bfloat16)
    project(loads, heads, w, outs, terms, out_sems)


def finish(place, lists, q, recv, o1, lse1, o2, lse2, weight):
    heads = jax.ShapeDtypeStruct((STEPS * ROWS, GROUPS * DH), jnp.bfloat16)
    heads, *terms = pl.pallas_call(
        finish_kernel,
        out_shape=(heads,) + TERMS,
        in_specs=[SMEM] + [ANY] * 8,
        out_specs=(VMEM,) + (ANY,) * TILES,
        scratch_shapes=[
            LISTS, QUERIES, pages_scratch(RECV), RESULT, LSE, QUERIES, LSE, LSE, RESULT, SCORES,
            pltpu.SemaphoreType.DMA((7,)),
        ] + PROJECT_SCRATCH,
        compiler_params=PARAMS,
        name="attend_merge_project",
    )(place, lists, q, recv, o1, lse1, o2, lse2, weight)
    return heads, terms


def project_kernel(place, heads, weight, *refs):
    outs, (w, terms, w_sems, out_sems) = refs[:TILES], refs[TILES:]
    project(start_tiles(place, 0, weight, w, w_sems), heads, w, outs, terms, out_sems)


def project_mine(place, heads, weight):
    return pl.pallas_call(
        project_kernel,
        out_shape=TERMS,
        in_specs=[SMEM, VMEM, ANY],
        out_specs=(ANY,) * TILES,
        scratch_shapes=PROJECT_SCRATCH,
        compiler_params=PARAMS,
        cost_estimate=pl.CostEstimate(flops=10**9, bytes_accessed=6 * 10**6, transcendentals=0),
        name="project_mine",
    )(place, heads, weight)


def sum_over_y(terms):
    total = terms[SHIFTS.index(0)].astype(jnp.float32)
    for term, shift in zip(terms, SHIFTS):
        if shift:
            moved = lax.ppermute(term, "ty", [(i, (i + shift) % 4) for i in range(4)])
            total = total + moved.astype(jnp.float32)
    return total


def page_lists(here, place, lengths, fresh=None):
    column = jnp.arange(MAXP, dtype=jnp.int32)[None, :]
    here = here & (column * PAGE < lengths[:, None])
    kept = here.astype(jnp.int32)
    rank = jnp.cumsum(kept, axis=1) - 1
    slot = jnp.arange(MAXP, dtype=jnp.int32)[None, :, None]
    chosen = here[:, None, :] & (rank[:, None, :] == slot)
    idx = jnp.sum(jnp.where(chosen, place[:, None, :], 0), axis=2)
    count = jnp.sum(kept, axis=1)
    tokens = jnp.sum(kept * jnp.minimum(PAGE, lengths[:, None] - column * PAGE), axis=1)
    if fresh is not None:
        idx = jnp.concatenate([fresh, idx], axis=1)
        count, tokens = count + 1, tokens + PAGE
    idx = jnp.pad(idx, ((0, 0), (0, POSITIONS - idx.shape[1])))
    return jnp.concatenate([idx.reshape(-1), count, tokens])


def local_lists(table, lengths):
    fresh = 1 + POOL + jnp.arange(ROWS, dtype=jnp.int32)[:, None]
    return page_lists(table < POOL, 1 + table, lengths, fresh)


def arrived_lists(table, lengths, half):
    prompt = table < POOL + N_INST * PCAP
    px, mx = table - POOL, table - (POOL + N_INST * PCAP)
    source = jnp.where(prompt, px // PCAP, mx // MCAP)
    rank = jnp.where(prompt, px % PCAP, PCAP + mx % MCAP)
    group = (source >> 3) * 4 + (source & 3)
    here = (table >= POOL) & (((source >> 2) & 1) == half)
    return page_lists(here, 1 + group * SLOTS + rank, lengths)


def per_device(
    queries,
    new_keys,
    new_values,
    pool_keys,
    pool_values,
    prompt_keys,
    prompt_values,
    moved_keys,
    moved_values,
    prompt_dest,
    moved_dest,
    block_table,
    context_len,
    out_weight,
):
    page = lambda x: x.reshape(x.shape[0], PAGE, DH)
    swap = [(0, 1), (1, 0)]
    half = lax.axis_index("izh")

    def exchange(send):
        send = send.reshape(N_HALF, SLOTS, 2, PAGE, DH)
        recv = lax.all_to_all(send, HALF, split_axis=0, concat_axis=0, tiled=True)
        return recv.reshape(RECV, 2, PAGE, DH)

    pages = (page(prompt_keys), page(prompt_values), page(moved_keys), page(moved_values))
    far_recv = exchange(pack((1 - half)[None], prompt_dest, moved_dest, *pages))
    q = queries.reshape(ROWS * QROWS, DH)
    far_q = lax.ppermute(q, "izh", swap)
    far_lists = lax.ppermute(arrived_lists(block_table, context_len, 1 - half), "izh", swap)
    near_lists = arrived_lists(block_table, context_len, half)

    fresh = jnp.stack([new_keys, new_values], axis=0).reshape(2, STEPS, ROWS, DH).transpose(2, 0, 1, 3)
    fresh = jnp.pad(fresh, ((0, 0), (0, 0), (0, PAGE - STEPS), (0, 0)))
    o1, lse1 = attend_local(local_lists(block_table, context_len), q, page(pool_keys), page(pool_values), fresh)
    near_send = pack(half[None], prompt_dest, moved_dest, *pages, lse1)
    near_recv = exchange(gate(near_send, far_q, far_lists, near_lists))

    o2, lse2 = attend_far(far_lists, far_q, far_recv)
    o2 = lax.ppermute(o2, "izh", swap)
    lse2 = lax.ppermute(lse2, "izh", swap)

    place = jnp.stack([lax.axis_index("ty"), lax.axis_index("tz")]).astype(jnp.int32)
    heads, terms = finish(place, near_lists, q, near_recv, o1, lse1, o2, lse2, out_weight)
    other = lax.ppermute(sum_over_y(terms).astype(jnp.bfloat16), "tz", swap)
    mine = sum_over_y(project_mine(place, heads, out_weight))
    return (mine + other.astype(jnp.float32)).astype(jnp.bfloat16).reshape(STEPS, ROWS, -1)


def solution(mesh):
    fine = Mesh(mesh.devices.reshape(SIZES), NAMES)
    in_specs = (
        P(None, INST, TP, None),
        P(None, INST, TP, None),
        P(None, INST, TP, None),
        P(INST, TP, None, None),
        P(INST, TP, None, None),
        P(INST, TP, None, None),
        P(INST, TP, None, None),
        P(INST, TP, None, None),
        P(INST, TP, None, None),
        P(INST),
        P(INST),
        P(INST, None),
        P(INST),
        P(TP, None),
    )
    return jax.shard_map(
        per_device, mesh=fine, in_specs=in_specs, out_specs=P(None, INST, TP), check_vma=False
    )
```

```python
import functools

import jax
import jax.numpy as jnp
from jax import lax
from jax.experimental import pallas as pl
from jax.experimental.pallas import tpu as pltpu
from jax.sharding import Mesh, PartitionSpec as P

NAMES = ("ix", "izh", "izl", "ic", "ty", "tz")
SIZES = (4, 2, 2, 2, 4, 2)
INST = ("ix", "izh", "izl", "ic")
HALF = ("ix", "izl", "ic")
TP = ("ty", "tz")

N_INST = 32
N_HALF = 16
STEPS, ROWS, GROUPS, DH = 4, 64, 8, 128
QROWS = STEPS * GROUPS
PAGE, MAXP = 16, 48
POOL, OUT, MIG = 192, 192, 96
PCAP, MCAP = 12, 6
SLOTS = PCAP + MCAP
RECV = N_HALF * SLOTS
NARROW = 8
WIDE = 16
WIDE_CHUNKS = 4
POSITIONS = WIDE * WIDE_CHUNKS
LIST = ROWS * (POSITIONS + 4)
LIST_ROWS = 40
TEAM = 4
TEAMS = ROWS // TEAM
LANES = TEAM * QROWS
SCALE = DH ** -0.5
VMEM_LIMIT = 63 * 1024 * 1024

SMEM = pl.BlockSpec(memory_space=pltpu.SMEM)
VMEM = pl.BlockSpec(memory_space=pltpu.VMEM)
ANY = pl.BlockSpec(memory_space=pl.ANY)
PARAMS = pltpu.CompilerParams(vmem_limit_bytes=VMEM_LIMIT)


def start_all(pairs, sems):
    copies = [pltpu.make_async_copy(src, dst, sems.at[n]) for n, (src, dst) in enumerate(pairs)]
    for copy in copies:
        copy.start()
    return copies


def wait_all(copies):
    for copy in copies:
        copy.wait()


def pack_kernel(half, pdest, mdest, pk, pv, mk, mv, *refs):
    out, pages, send, pdest_s, mdest_s, slots, count, sems, out_sem = refs[-9:]
    loads = start_all(
        [
            (pdest, pdest_s),
            (mdest, mdest_s),
            (pk, pages.at[pl.ds(0, OUT), 0]),
            (pv, pages.at[pl.ds(0, OUT), 1]),
            (mk, pages.at[pl.ds(OUT, MIG), 0]),
            (mv, pages.at[pl.ds(OUT, MIG), 1]),
        ],
        sems,
    )
    wanted = half[0]
    for d in range(N_INST):
        count[d] = 0
        count[N_INST + d] = PCAP
    wait_all(loads[:2])

    def rank(dest, kind, first, j, carry):
        d = dest[j]
        k = count[kind + d]
        count[kind + d] = k + 1
        group = (d >> 3) * 4 + (d & 3)
        slots[first + j] = jnp.where(((d >> 2) & 1) == wanted, group * SLOTS + k, RECV)
        return carry

    def copy_page(j, carry):
        send[slots[j]] = pages[j]
        return carry

    lax.fori_loop(0, OUT, functools.partial(rank, pdest_s, 0, 0), 0, unroll=8)
    lax.fori_loop(0, MIG, functools.partial(rank, mdest_s, N_INST, OUT), 0, unroll=8)
    wait_all(loads[2:])
    lax.fori_loop(0, OUT + MIG, copy_page, 0, unroll=8)
    wait_all(start_all([(send.at[pl.ds(0, RECV)], out)], out_sem))


def pack(half, pdest, mdest, pk, pv, mk, mv, *after):
    return pl.pallas_call(
        pack_kernel,
        out_shape=jax.ShapeDtypeStruct((RECV, 2, PAGE, DH), jnp.bfloat16),
        in_specs=[SMEM] + [ANY] * (6 + len(after)),
        out_specs=ANY,
        scratch_shapes=[
            pltpu.VMEM((OUT + MIG, 2, PAGE, DH), jnp.bfloat16),
            pltpu.VMEM((RECV + 1, 2, PAGE, DH), jnp.bfloat16),
            pltpu.SMEM((OUT,), jnp.int32),
            pltpu.SMEM((MIG,), jnp.int32),
            pltpu.SMEM((OUT + MIG,), jnp.int32),
            pltpu.SMEM((2 * N_INST,), jnp.int32),
            pltpu.SemaphoreType.DMA((6,)),
            pltpu.SemaphoreType.DMA((1,)),
        ],
        compiler_params=PARAMS,
        cost_estimate=pl.CostEstimate(flops=10**6, bytes_accessed=10**7, transcendentals=0),
        name="pack_pages",
    )(half, pdest, mdest, pk, pv, mk, mv, *after)


def gate_kernel(x, *refs):
    pass


def gate(x, *after):
    return pl.pallas_call(
        gate_kernel,
        out_shape=jax.ShapeDtypeStruct(x.shape, x.dtype),
        in_specs=[ANY] * (1 + len(after)),
        out_specs=ANY,
        input_output_aliases={0: 0},
        name="gate",
    )(x, *after)


def attention(fresh, lists, q, kv, out, lse, scores):
    lane = lax.broadcasted_iota(jnp.int32, (1, LANES), 1)
    team_row = (lane // GROUPS) % TEAM
    step = lane // (TEAM * GROUPS)

    def entry(i):
        return lists[i // DH, i % DH] if isinstance(i, int) else lists[i >> 7, i & 127]

    def load(r, first, n, which):
        return [kv[entry(r * POSITIONS + first + p), which] for p in range(n)]

    def count(r):
        return entry(ROWS * POSITIONS + r)

    def tokens(r):
        return entry(ROWS * (POSITIONS + 1) + r)

    def team(t, g):
        first = t * ROWS * GROUPS + g * TEAM * GROUPS
        return pl.ds(first if isinstance(g, int) else pl.multiple_of(first, TEAM * GROUPS), TEAM * GROUPS)

    def queries(g):
        return jnp.concatenate([q[team(t, g), :] for t in range(STEPS)], axis=0)

    def mask(s, first, limit):
        token = lax.broadcasted_iota(jnp.int32, s.shape, 0) + first
        seen = token < limit
        if fresh:
            seen = token < jnp.where(token < PAGE, step + 1, limit)
        return jnp.where(seen, s * SCALE, -jnp.inf)

    def dot_nt(a, b):
        return lax.dot_general(a, b, (((1,), (1,)), ((), ())), preferred_element_type=jnp.float32)

    def narrow(g):
        width = NARROW * PAGE
        rows = [g * TEAM + i for i in range(TEAM)]
        keys = jnp.concatenate([k for r in rows for k in load(r, 0, NARROW, 0)], axis=0)
        s_all = dot_nt(keys, queries(g))
        s = s_all[:width]
        limit = jnp.full((1, LANES), tokens(rows[0]), jnp.int32)
        owner = (lax.broadcasted_iota(jnp.int32, (width, LANES), 1) // GROUPS) % TEAM
        for i in range(1, TEAM):
            s = jnp.where(owner == i, s_all[i * width : (i + 1) * width], s)
            limit = jnp.where(team_row == i, tokens(rows[i]), limit)
        s = mask(s, 0, limit)
        m = jnp.maximum(jnp.max(s, axis=0, keepdims=True), -1e30)
        e = jnp.exp(s - m)
        total = jnp.sum(e, axis=0, keepdims=True)
        safe = jnp.maximum(total, 1e-30)
        lse[pl.ds(g, 1), :] = jnp.where(total > 0.0, m + jnp.log(safe), -1e30)
        weights = (e * (1.0 / safe)).T
        for i in range(TEAM):
            values = jnp.concatenate(load(rows[i], 0, NARROW, 1), axis=0)
            pieces = [weights[(t * TEAM + i) * GROUPS : (t * TEAM + i + 1) * GROUPS] for t in range(STEPS)]
            part = jnp.concatenate(pieces, axis=0).astype(jnp.bfloat16)
            product = jnp.dot(part, values, preferred_element_type=jnp.float32)
            for t in range(STEPS):
                first = (t * ROWS + rows[i]) * GROUPS
                out[pl.ds(first, GROUPS), :] = product[t * GROUPS : (t + 1) * GROUPS]

    for g in range(TEAMS):
        narrow(g)

    def put(r, product, m, total, safe):
        g, i = r // TEAM, r % TEAM
        size = TEAM * GROUPS
        owner = lax.broadcasted_iota(jnp.int32, (size, DH), 0) // GROUPS
        for t in range(STEPS):
            rows = team(t, g)
            out[rows, :] = jnp.where(owner == i, product[t * size : (t + 1) * size], out[rows, :])
        new = jnp.where(total > 0.0, m + jnp.log(safe), -1e30)
        lse[pl.ds(g, 1), :] = jnp.where(team_row == i, new, lse[pl.ds(g, 1), :])

    def chunk_scores(r, c):
        keys = jnp.concatenate(load(r, c * WIDE, WIDE, 0), axis=0)
        return mask(dot_nt(keys, queries(r // TEAM)), c * WIDE * PAGE, tokens(r))

    def chunk_out(r, c, weights):
        values = jnp.concatenate(load(r, c * WIDE, WIDE, 1), axis=0)
        return jnp.dot(weights.T.astype(jnp.bfloat16), values, preferred_element_type=jnp.float32)

    def one_chunk(r):
        s = chunk_scores(r, 0)
        m = jnp.maximum(jnp.max(s, axis=0, keepdims=True), -1e30)
        e = jnp.exp(s - m)
        total = jnp.sum(e, axis=0, keepdims=True)
        safe = jnp.maximum(total, 1e-30)
        put(r, chunk_out(r, 0, e * (1.0 / safe)), m, total, safe)

    def more_chunks(r):
        chunks = (count(r) + WIDE - 1) // WIDE

        def first_pass(c, m):
            s = chunk_scores(r, c)
            scores[c] = s
            return jnp.maximum(m, jnp.max(s, axis=0, keepdims=True))

        m = lax.fori_loop(0, chunks, first_pass, jnp.full((1, LANES), -1e30, jnp.float32))

        def second_pass(c, total):
            e = jnp.exp(scores[c] - m)
            scores[c] = e
            return total + jnp.sum(e, axis=0, keepdims=True)

        total = lax.fori_loop(0, chunks, second_pass, jnp.zeros((1, LANES), jnp.float32))
        safe = jnp.maximum(total, 1e-30)
        inverse = 1.0 / safe

        def third_pass(c, product):
            return product + chunk_out(r, c, scores[c] * inverse)

        product = lax.fori_loop(0, chunks, third_pass, jnp.zeros((LANES, DH), jnp.float32))
        put(r, product, m, total, safe)

    def wide_body(k, carry):
        r = entry(ROWS * (POSITIONS + 2) + k)
        pl.when(count(r) <= WIDE)(lambda: one_chunk(r))
        pl.when(count(r) > WIDE)(lambda: more_chunks(r))
        return carry

    lax.fori_loop(0, entry(ROWS * (POSITIONS + 3)), wide_body, 0)


QUERIES = pltpu.VMEM((ROWS * QROWS, DH), jnp.bfloat16)
SCORES = pltpu.VMEM((WIDE_CHUNKS, WIDE * PAGE, LANES), jnp.float32)
RESULT = pltpu.VMEM((ROWS * QROWS, DH), jnp.float32)
LSE = pltpu.VMEM((TEAMS, LANES), jnp.float32)
LISTS = pltpu.SMEM((LIST_ROWS, DH), jnp.int32)


def pages_scratch(n):
    return pltpu.VMEM((1 + n, 2, PAGE, DH), jnp.bfloat16)


def blank_page():
    return jnp.zeros((2, PAGE, DH), jnp.bfloat16)


def attend_local_kernel(lists, q, pool_k, pool_v, fresh, after, out, lse, lists_s, q_s, kv, scores, sems):
    copies = start_all(
        [
            (lists, lists_s),
            (q, q_s),
            (pool_k, kv.at[pl.ds(1, POOL), 0]),
            (pool_v, kv.at[pl.ds(1, POOL), 1]),
            (fresh, kv.at[pl.ds(1 + POOL, ROWS)]),
        ],
        sems,
    )
    kv[0] = blank_page()
    wait_all(copies)
    attention(True, lists_s, q_s, kv, out, lse, scores)


def attend_local(lists, q, pool_k, pool_v, fresh, after):
    return pl.pallas_call(
        attend_local_kernel,
        out_shape=(
            jax.ShapeDtypeStruct((ROWS * QROWS, DH), jnp.float32),
            jax.ShapeDtypeStruct((TEAMS, LANES), jnp.float32),
        ),
        in_specs=[ANY] * 6,
        out_specs=(VMEM, VMEM),
        scratch_shapes=[LISTS, QUERIES, pages_scratch(POOL + ROWS), SCORES, pltpu.SemaphoreType.DMA((5,))],
        compiler_params=PARAMS,
        cost_estimate=pl.CostEstimate(flops=10**11, bytes_accessed=10**8, transcendentals=10**6),
        name="attend_local",
    )(lists, q, pool_k, pool_v, fresh, after)


def attend_far_kernel(letter, recv, out, lse, lists_s, lists_v, coded, q_s, kv, result, scores, sems):
    copies = start_all(
        [
            (letter.at[pl.ds(ROWS * QROWS, 2 * LIST_ROWS)], coded),
            (letter.at[pl.ds(0, ROWS * QROWS)], q_s),
            (recv, kv.at[pl.ds(1, RECV)]),
        ],
        sems,
    )
    kv[0] = blank_page()
    copies[0].wait()
    numbers = coded[...].astype(jnp.float32)
    lists_v[...] = (numbers[:LIST_ROWS] * 256.0 + numbers[LIST_ROWS:]).astype(jnp.int32)
    lists_copy = pltpu.make_async_copy(lists_v, lists_s, sems.at[3])
    lists_copy.start()
    lists_copy.wait()
    wait_all(copies[1:])
    attention(False, lists_s, q_s, kv, result, lse, scores)
    out[...] = result[...].astype(jnp.bfloat16)


def attend_far(letter, recv):
    return pl.pallas_call(
        attend_far_kernel,
        out_shape=(
            jax.ShapeDtypeStruct((ROWS * QROWS, DH), jnp.bfloat16),
            jax.ShapeDtypeStruct((TEAMS, LANES), jnp.float32),
        ),
        in_specs=[ANY] * 2,
        out_specs=(VMEM, VMEM),
        scratch_shapes=[
            LISTS,
            pltpu.VMEM((LIST_ROWS, DH), jnp.int32),
            pltpu.VMEM((2 * LIST_ROWS, DH), jnp.bfloat16),
            QUERIES,
            pages_scratch(RECV),
            RESULT,
            SCORES,
            pltpu.SemaphoreType.DMA((4,)),
        ],
        compiler_params=PARAMS,
        cost_estimate=pl.CostEstimate(flops=10**11, bytes_accessed=10**8, transcendentals=10**6),
        name="attend_far",
    )(letter, recv)


SHIFTS = (2, 1, 3, 0)
BLOCK = 512


def column_tile(place, side, shift, weight):
    y = lax.rem(place[0] + shift, 4)
    z = place[1] if side == 0 else 1 - place[1]
    return weight.at[:, pl.ds(pl.multiple_of((y * 2 + z) * BLOCK, BLOCK), BLOCK)]


def start_tiles(place, side, weight, w, w_sems):
    loads = [
        pltpu.make_async_copy(column_tile(place, side, shift, weight), w.at[n], w_sems.at[n])
        for n, shift in enumerate(SHIFTS)
    ]
    for load in loads:
        load.start()
    return loads


def project(loads, heads, w, outs, terms, out_sems):
    stores = []
    for n, load in enumerate(loads):
        load.wait()
        terms[n] = jnp.dot(heads[...], w[n], preferred_element_type=jnp.float32).astype(jnp.bfloat16)
        store = pltpu.make_async_copy(terms.at[n], outs[n], out_sems.at[n])
        store.start()
        stores.append(store)
    for store in stores:
        store.wait()


TILES = len(SHIFTS)
TERMS = (jax.ShapeDtypeStruct((STEPS * ROWS, BLOCK), jnp.bfloat16),) * TILES
PROJECT_SCRATCH = [
    pltpu.VMEM((TILES, GROUPS * DH, BLOCK), jnp.bfloat16),
    pltpu.VMEM((TILES, STEPS * ROWS, BLOCK), jnp.bfloat16),
    pltpu.SemaphoreType.DMA((TILES,)),
    pltpu.SemaphoreType.DMA((TILES,)),
]


def finish_kernel(place, lists, q, recv, o1, lse1, o2, lse2, weight, heads, *refs):
    outs, refs = refs[:TILES], refs[TILES:]
    lists_s, q_s, kv, o1_s, lse1_s, o2_s, lse2_s, lse3, result, scores, sems, part_sems, w, terms, w_sems, out_sems = refs
    copies = start_all([(lists, lists_s), (q, q_s), (recv, kv.at[pl.ds(1, RECV)])], sems)
    parts = start_all([(lse1, lse1_s), (lse2, lse2_s), (o1, o1_s), (o2, o2_s)], part_sems)
    kv[0] = blank_page()
    wait_all(copies)
    loads = start_tiles(place, 1, weight, w, w_sems)
    attention(False, lists_s, q_s, kv, result, lse3, scores)
    wait_all(parts)

    top = jnp.maximum(jnp.maximum(lse1_s[...], lse2_s[...]), lse3[...])
    parts = [jnp.exp(x[...] - top) for x in (lse1_s, lse2_s, lse3)]
    inverse = 1.0 / (parts[0] + parts[1] + parts[2])
    f1, f2, f3 = [(x * inverse).T for x in parts]
    size = TEAM * GROUPS
    for t in range(STEPS):
        for g in range(TEAMS):
            rows = pl.ds((t * TEAMS + g) * size, size)
            lanes = slice(t * size, (t + 1) * size)
            merged = f1[lanes, g : g + 1] * o1_s[rows, :] + f2[lanes, g : g + 1] * o2_s[rows, :].astype(jnp.float32)
            result[rows, :] = merged + f3[lanes, g : g + 1] * result[rows, :]
        for h in range(GROUPS):
            column = result[pl.ds(t * ROWS * GROUPS + h, ROWS, stride=GROUPS), :]
            heads[pl.ds(t * ROWS, ROWS), pl.ds(h * DH, DH)] = column.astype(jnp.bfloat16)
    project(loads, heads, w, outs, terms, out_sems)


def finish(place, lists, q, recv, o1, lse1, o2, lse2, weight):
    heads = jax.ShapeDtypeStruct((STEPS * ROWS, GROUPS * DH), jnp.bfloat16)
    heads, *terms = pl.pallas_call(
        finish_kernel,
        out_shape=(heads,) + TERMS,
        in_specs=[SMEM] + [ANY] * 8,
        out_specs=(VMEM,) + (ANY,) * TILES,
        scratch_shapes=[
            LISTS, QUERIES, pages_scratch(RECV), RESULT, LSE, QUERIES, LSE, LSE, RESULT, SCORES,
            pltpu.SemaphoreType.DMA((3,)),
            pltpu.SemaphoreType.DMA((4,)),
        ] + PROJECT_SCRATCH,
        compiler_params=PARAMS,
        name="attend_merge_project",
    )(place, lists, q, recv, o1, lse1, o2, lse2, weight)
    return heads, terms


def project_kernel(place, heads, weight, *refs):
    outs, (w, terms, w_sems, out_sems) = refs[:TILES], refs[TILES:]
    project(start_tiles(place, 0, weight, w, w_sems), heads, w, outs, terms, out_sems)


def project_mine(place, heads, weight):
    return pl.pallas_call(
        project_kernel,
        out_shape=TERMS,
        in_specs=[SMEM, VMEM, ANY],
        out_specs=(ANY,) * TILES,
        scratch_shapes=PROJECT_SCRATCH,
        compiler_params=PARAMS,
        cost_estimate=pl.CostEstimate(flops=10**9, bytes_accessed=6 * 10**6, transcendentals=0),
        name="project_mine",
    )(place, heads, weight)


def sum_over_y(terms):
    total = terms[SHIFTS.index(0)].astype(jnp.float32)
    for term, shift in zip(terms, SHIFTS):
        if shift:
            moved = lax.ppermute(term, "ty", [(i, (i + shift) % 4) for i in range(4)])
            total = total + moved.astype(jnp.float32)
    return total


def page_lists(here, place, lengths, fresh=None):
    column = jnp.arange(MAXP, dtype=jnp.int32)[None, :]
    here = here & (column * PAGE < lengths[:, None])
    kept = here.astype(jnp.int32)
    rank = jnp.cumsum(kept, axis=1) - 1
    slot = jnp.arange(MAXP, dtype=jnp.int32)[None, :, None]
    chosen = here[:, None, :] & (rank[:, None, :] == slot)
    idx = jnp.sum(jnp.where(chosen, place[:, None, :], 0), axis=2)
    count = jnp.sum(kept, axis=1)
    tokens = jnp.sum(kept * jnp.minimum(PAGE, lengths[:, None] - column * PAGE), axis=1)
    if fresh is not None:
        idx = jnp.concatenate([fresh, idx], axis=1)
        count, tokens = count + 1, tokens + PAGE
    idx = jnp.pad(idx, ((0, 0), (0, POSITIONS - idx.shape[1])))
    wide = count > NARROW
    place_of = jnp.cumsum(wide.astype(jnp.int32)) - 1
    row = jnp.arange(ROWS, dtype=jnp.int32)
    picked = wide[None, :] & (place_of[None, :] == row[:, None])
    wide_rows = jnp.sum(jnp.where(picked, row[None, :], 0), axis=1)
    wide_count = jnp.broadcast_to(jnp.sum(wide.astype(jnp.int32)), (ROWS,))
    spare = jnp.zeros((LIST_ROWS * DH - LIST,), jnp.int32)
    return jnp.concatenate([idx.reshape(-1), count, tokens, wide_rows, wide_count, spare]).reshape(LIST_ROWS, DH)


def local_lists(table, lengths):
    fresh = 1 + POOL + jnp.arange(ROWS, dtype=jnp.int32)[:, None]
    return page_lists(table < POOL, 1 + table, lengths, fresh)


def arrived_lists(table, lengths, half):
    prompt = table < POOL + N_INST * PCAP
    px, mx = table - POOL, table - (POOL + N_INST * PCAP)
    source = jnp.where(prompt, px // PCAP, mx // MCAP)
    rank = jnp.where(prompt, px % PCAP, PCAP + mx % MCAP)
    group = (source >> 3) * 4 + (source & 3)
    here = (table >= POOL) & (((source >> 2) & 1) == half)
    return page_lists(here, 1 + group * SLOTS + rank, lengths)


def as_rows(lists):
    return jnp.concatenate([lists >> 8, lists & 255], axis=0).astype(jnp.bfloat16)


def per_device(
    queries,
    new_keys,
    new_values,
    pool_keys,
    pool_values,
    prompt_keys,
    prompt_values,
    moved_keys,
    moved_values,
    prompt_dest,
    moved_dest,
    block_table,
    context_len,
    out_weight,
):
    page = lambda x: x.reshape(x.shape[0], PAGE, DH)
    swap = [(0, 1), (1, 0)]
    half = lax.axis_index("izh")

    def exchange(send):
        send = send.reshape(N_HALF, SLOTS, 2, PAGE, DH)
        recv = lax.all_to_all(send, HALF, split_axis=0, concat_axis=0, tiled=True)
        return recv.reshape(RECV, 2, PAGE, DH)

    pages = (page(prompt_keys), page(prompt_values), page(moved_keys), page(moved_values))
    far_recv = exchange(pack((1 - half)[None], prompt_dest, moved_dest, *pages))
    q = queries.reshape(ROWS * QROWS, DH)
    letter = jnp.concatenate([q, as_rows(arrived_lists(block_table, context_len, 1 - half))], axis=0)
    near_lists = arrived_lists(block_table, context_len, half)
    near_send = pack(half[None], prompt_dest, moved_dest, *pages, near_lists)
    fresh = jnp.stack([new_keys, new_values], axis=0).reshape(2, STEPS, ROWS, DH).transpose(2, 0, 1, 3)
    fresh = jnp.pad(fresh, ((0, 0), (0, 0), (0, PAGE - STEPS), (0, 0)))
    local_pages = (page(pool_keys), page(pool_values), fresh)
    local = local_lists(block_table, context_len)
    o1, lse1 = attend_local(local, q, *local_pages, near_send)
    letter = lax.ppermute(gate(letter, lse1), "izh", swap)
    near_recv = exchange(near_send)

    o2, lse2 = attend_far(letter, far_recv)
    o2 = lax.ppermute(o2, "izh", swap)
    lse2 = lax.ppermute(lse2, "izh", swap)

    place = jnp.stack([lax.axis_index("ty"), lax.axis_index("tz")]).astype(jnp.int32)
    heads, terms = finish(place, near_lists, q, near_recv, o1, lse1, o2, lse2, out_weight)
    other = lax.ppermute(sum_over_y(terms).astype(jnp.bfloat16), "tz", swap)
    mine = sum_over_y(project_mine(place, heads, out_weight))
    return (mine + other.astype(jnp.float32)).astype(jnp.bfloat16).reshape(STEPS, ROWS, -1)


def solution(mesh):
    fine = Mesh(mesh.devices.reshape(SIZES), NAMES)
    in_specs = (
        P(None, INST, TP, None),
        P(None, INST, TP, None),
        P(None, INST, TP, None),
        P(INST, TP, None, None),
        P(INST, TP, None, None),
        P(INST, TP, None, None),
        P(INST, TP, None, None),
        P(INST, TP, None, None),
        P(INST, TP, None, None),
        P(INST),
        P(INST),
        P(INST, None),
        P(INST),
        P(TP, None),
    )
    return jax.shard_map(
        per_device, mesh=fine, in_specs=in_specs, out_specs=P(None, INST, TP), check_vma=False
    )
```

```python
import functools

import jax
import jax.numpy as jnp
from jax import lax
from jax.experimental import pallas as pl
from jax.experimental.pallas import tpu as pltpu
from jax.sharding import Mesh, PartitionSpec as P

NAMES = ("ix", "izh", "izl", "ic", "ty", "tz")
SIZES = (4, 2, 2, 2, 4, 2)
INST = ("ix", "izh", "izl", "ic")
HALF = ("ix", "izl", "ic")
TP = ("ty", "tz")

N_INST = 32
N_HALF = 16
STEPS, ROWS, GROUPS, DH = 4, 64, 8, 128
QROWS = STEPS * GROUPS
PAGE, MAXP = 16, 48
POOL, OUT, MIG = 192, 192, 96
PCAP, MCAP = 12, 6
SLOTS = PCAP + MCAP
RECV = N_HALF * SLOTS
NARROW = 8
WIDE = 16
WIDE_CHUNKS = 4
POSITIONS = WIDE * WIDE_CHUNKS
LIST = ROWS * (POSITIONS + 4)
LIST_ROWS = 40
PIECES = 6
TEAM = 4
TEAMS = ROWS // TEAM
LANES = TEAM * QROWS
SCALE = DH ** -0.5
VMEM_LIMIT = 62 * 1024 * 1024

SMEM = pl.BlockSpec(memory_space=pltpu.SMEM)
VMEM = pl.BlockSpec(memory_space=pltpu.VMEM)
ANY = pl.BlockSpec(memory_space=pl.ANY)
PARAMS = pltpu.CompilerParams(vmem_limit_bytes=VMEM_LIMIT)


def start_all(pairs, sems):
    copies = [pltpu.make_async_copy(src, dst, sems.at[n]) for n, (src, dst) in enumerate(pairs)]
    for copy in copies:
        copy.start()
    return copies


def wait_all(copies):
    for copy in copies:
        copy.wait()


def pack_kernel(half, pdest, mdest, pk, pv, mk, mv, *refs):
    out, pages, send, pdest_s, mdest_s, chosen, count, sems, out_sems = refs[-9:]
    loads = start_all(
        [
            (pdest, pdest_s),
            (mdest, mdest_s),
            (pk, pages.at[pl.ds(0, OUT), 0]),
            (pv, pages.at[pl.ds(0, OUT), 1]),
            (mk, pages.at[pl.ds(OUT, MIG), 0]),
            (mv, pages.at[pl.ds(OUT, MIG), 1]),
        ],
        sems,
    )
    wanted = half[0]
    for d in range(N_INST):
        count[d] = 0
        count[N_INST + d] = PCAP

    def clear(n, carry):
        chosen[n] = 0
        return carry

    lax.fori_loop(0, RECV, clear, 0, unroll=8)
    wait_all(loads[:2])

    def rank(dest, kind, first, j, carry):
        d = dest[j]
        k = count[kind + d]
        count[kind + d] = k + 1
        group = (d >> 3) * 4 + (d & 3)
        chosen[jnp.where(((d >> 2) & 1) == wanted, group * SLOTS + k, RECV)] = first + j
        return carry

    def copy_page(n, carry):
        send[n] = pages[chosen[n]]
        return carry

    lax.fori_loop(0, OUT, functools.partial(rank, pdest_s, 0, 0), 0, unroll=8)
    lax.fori_loop(0, MIG, functools.partial(rank, mdest_s, N_INST, OUT), 0, unroll=8)
    wait_all(loads[2:])
    stores = []
    for n in range(PIECES):
        piece = pl.ds(n * (RECV // PIECES), RECV // PIECES)
        lax.fori_loop(n * (RECV // PIECES), (n + 1) * (RECV // PIECES), copy_page, 0, unroll=8)
        stores += start_all([(send.at[piece], out.at[piece])], out_sems.at[pl.ds(n, 1)])
    wait_all(stores)


def pack(half, pdest, mdest, pk, pv, mk, mv, *after):
    return pl.pallas_call(
        pack_kernel,
        out_shape=jax.ShapeDtypeStruct((RECV, 2, PAGE, DH), jnp.bfloat16),
        in_specs=[SMEM] + [ANY] * (6 + len(after)),
        out_specs=ANY,
        scratch_shapes=[
            pltpu.VMEM((OUT + MIG, 2, PAGE, DH), jnp.bfloat16),
            pltpu.VMEM((RECV, 2, PAGE, DH), jnp.bfloat16),
            pltpu.SMEM((OUT,), jnp.int32),
            pltpu.SMEM((MIG,), jnp.int32),
            pltpu.SMEM((RECV + 1,), jnp.int32),
            pltpu.SMEM((2 * N_INST,), jnp.int32),
            pltpu.SemaphoreType.DMA((6,)),
            pltpu.SemaphoreType.DMA((PIECES,)),
        ],
        compiler_params=PARAMS,
        cost_estimate=pl.CostEstimate(flops=10**6, bytes_accessed=10**7, transcendentals=0),
        name="pack_pages",
    )(half, pdest, mdest, pk, pv, mk, mv, *after)


def gate_kernel(x, *refs):
    pass


def gate(x, *after):
    return pl.pallas_call(
        gate_kernel,
        out_shape=jax.ShapeDtypeStruct(x.shape, x.dtype),
        in_specs=[ANY] * (1 + len(after)),
        out_specs=ANY,
        input_output_aliases={0: 0},
        name="gate",
    )(x, *after)


def attention(fresh, lists, q, kv, out, lse, scores):
    lane = lax.broadcasted_iota(jnp.int32, (1, LANES), 1)
    team_row = (lane // GROUPS) % TEAM
    step = lane // (TEAM * GROUPS)

    def entry(i):
        return lists[i // DH, i % DH] if isinstance(i, int) else lists[i >> 7, i & 127]

    def load(r, first, n, which):
        return [kv[entry(r * POSITIONS + first + p), which] for p in range(n)]

    def count(r):
        return entry(ROWS * POSITIONS + r)

    def tokens(r):
        return entry(ROWS * (POSITIONS + 1) + r)

    def team(t, g):
        first = t * ROWS * GROUPS + g * TEAM * GROUPS
        return pl.ds(first if isinstance(g, int) else pl.multiple_of(first, TEAM * GROUPS), TEAM * GROUPS)

    def queries(g):
        return jnp.concatenate([q[team(t, g), :] for t in range(STEPS)], axis=0)

    def mask(s, first, limit):
        token = lax.broadcasted_iota(jnp.int32, s.shape, 0) + first
        seen = token < limit
        if fresh:
            seen = token < jnp.where(token < PAGE, step + 1, limit)
        return jnp.where(seen, s * SCALE, -jnp.inf)

    def dot_nt(a, b):
        return lax.dot_general(a, b, (((1,), (1,)), ((), ())), preferred_element_type=jnp.float32)

    def narrow(g):
        width = NARROW * PAGE
        rows = [g * TEAM + i for i in range(TEAM)]
        keys = jnp.concatenate([k for r in rows for k in load(r, 0, NARROW, 0)], axis=0)
        s_all = dot_nt(keys, queries(g))
        s = s_all[:width]
        limit = jnp.full((1, LANES), tokens(rows[0]), jnp.int32)
        owner = (lax.broadcasted_iota(jnp.int32, (width, LANES), 1) // GROUPS) % TEAM
        for i in range(1, TEAM):
            s = jnp.where(owner == i, s_all[i * width : (i + 1) * width], s)
            limit = jnp.where(team_row == i, tokens(rows[i]), limit)
        s = mask(s, 0, limit)
        m = jnp.maximum(jnp.max(s, axis=0, keepdims=True), -1e30)
        e = jnp.exp(s - m)
        total = jnp.sum(e, axis=0, keepdims=True)
        safe = jnp.maximum(total, 1e-30)
        lse[pl.ds(g, 1), :] = jnp.where(total > 0.0, m + jnp.log(safe), -1e30)
        weights = (e * (1.0 / safe)).T
        for i in range(TEAM):
            values = jnp.concatenate(load(rows[i], 0, NARROW, 1), axis=0)
            pieces = [weights[(t * TEAM + i) * GROUPS : (t * TEAM + i + 1) * GROUPS] for t in range(STEPS)]
            part = jnp.concatenate(pieces, axis=0).astype(jnp.bfloat16)
            product = jnp.dot(part, values, preferred_element_type=jnp.float32)
            for t in range(STEPS):
                first = (t * ROWS + rows[i]) * GROUPS
                out[pl.ds(first, GROUPS), :] = product[t * GROUPS : (t + 1) * GROUPS]

    for g in range(TEAMS):
        narrow(g)

    def put(r, product, m, total, safe):
        g, i = r // TEAM, r % TEAM
        size = TEAM * GROUPS
        owner = lax.broadcasted_iota(jnp.int32, (size, DH), 0) // GROUPS
        for t in range(STEPS):
            rows = team(t, g)
            out[rows, :] = jnp.where(owner == i, product[t * size : (t + 1) * size], out[rows, :])
        new = jnp.where(total > 0.0, m + jnp.log(safe), -1e30)
        lse[pl.ds(g, 1), :] = jnp.where(team_row == i, new, lse[pl.ds(g, 1), :])

    def chunk_scores(r, c):
        keys = jnp.concatenate(load(r, c * WIDE, WIDE, 0), axis=0)
        return mask(dot_nt(keys, queries(r // TEAM)), c * WIDE * PAGE, tokens(r))

    def chunk_out(r, c, weights):
        values = jnp.concatenate(load(r, c * WIDE, WIDE, 1), axis=0)
        return jnp.dot(weights.T.astype(jnp.bfloat16), values, preferred_element_type=jnp.float32)

    def one_chunk(r):
        s = chunk_scores(r, 0)
        m = jnp.maximum(jnp.max(s, axis=0, keepdims=True), -1e30)
        e = jnp.exp(s - m)
        total = jnp.sum(e, axis=0, keepdims=True)
        safe = jnp.maximum(total, 1e-30)
        put(r, chunk_out(r, 0, e * (1.0 / safe)), m, total, safe)

    def more_chunks(r):
        chunks = (count(r) + WIDE - 1) // WIDE

        def first_pass(c, m):
            s = chunk_scores(r, c)
            scores[c] = s
            return jnp.maximum(m, jnp.max(s, axis=0, keepdims=True))

        m = lax.fori_loop(0, chunks, first_pass, jnp.full((1, LANES), -1e30, jnp.float32))

        def second_pass(c, total):
            e = jnp.exp(scores[c] - m)
            scores[c] = e
            return total + jnp.sum(e, axis=0, keepdims=True)

        total = lax.fori_loop(0, chunks, second_pass, jnp.zeros((1, LANES), jnp.float32))
        safe = jnp.maximum(total, 1e-30)
        inverse = 1.0 / safe

        def third_pass(c, product):
            return product + chunk_out(r, c, scores[c] * inverse)

        product = lax.fori_loop(0, chunks, third_pass, jnp.zeros((LANES, DH), jnp.float32))
        put(r, product, m, total, safe)

    def wide_body(k, carry):
        r = entry(ROWS * (POSITIONS + 2) + k)
        pl.when(count(r) <= WIDE)(lambda: one_chunk(r))
        pl.when(count(r) > WIDE)(lambda: more_chunks(r))
        return carry

    lax.fori_loop(0, entry(ROWS * (POSITIONS + 3)), wide_body, 0)


QUERIES = pltpu.VMEM((ROWS * QROWS, DH), jnp.bfloat16)
SCORES = pltpu.VMEM((WIDE_CHUNKS, WIDE * PAGE, LANES), jnp.float32)
RESULT = pltpu.VMEM((ROWS * QROWS, DH), jnp.float32)
LSE = pltpu.VMEM((TEAMS, LANES), jnp.float32)
LISTS = pltpu.SMEM((LIST_ROWS, DH), jnp.int32)


def pages_scratch(n):
    return pltpu.VMEM((1 + n, 2, PAGE, DH), jnp.bfloat16)


def blank_page():
    return jnp.zeros((2, PAGE, DH), jnp.bfloat16)


def attend_local_kernel(lists, q, pool_k, pool_v, fresh, after, out, lse, lists_s, q_s, kv, scores, sems):
    copies = start_all(
        [
            (lists, lists_s),
            (q, q_s),
            (pool_k, kv.at[pl.ds(1, POOL), 0]),
            (pool_v, kv.at[pl.ds(1, POOL), 1]),
            (fresh, kv.at[pl.ds(1 + POOL, ROWS)]),
        ],
        sems,
    )
    kv[0] = blank_page()
    wait_all(copies)
    attention(True, lists_s, q_s, kv, out, lse, scores)


def attend_local(lists, q, pool_k, pool_v, fresh, after):
    return pl.pallas_call(
        attend_local_kernel,
        out_shape=(
            jax.ShapeDtypeStruct((ROWS * QROWS, DH), jnp.float32),
            jax.ShapeDtypeStruct((TEAMS, LANES), jnp.float32),
        ),
        in_specs=[ANY] * 6,
        out_specs=(VMEM, VMEM),
        scratch_shapes=[LISTS, QUERIES, pages_scratch(POOL + ROWS), SCORES, pltpu.SemaphoreType.DMA((5,))],
        compiler_params=PARAMS,
        cost_estimate=pl.CostEstimate(flops=10**11, bytes_accessed=10**8, transcendentals=10**6),
        name="attend_local",
    )(lists, q, pool_k, pool_v, fresh, after)


def attend_far_kernel(letter, recv, out, lse, lists_s, lists_v, coded, q_s, kv, result, scores, sems):
    copies = start_all(
        [
            (letter.at[pl.ds(ROWS * QROWS, 2 * LIST_ROWS)], coded),
            (letter.at[pl.ds(0, ROWS * QROWS)], q_s),
            (recv, kv.at[pl.ds(1, RECV)]),
        ],
        sems,
    )
    kv[0] = blank_page()
    copies[0].wait()
    numbers = coded[...].astype(jnp.float32)
    lists_v[...] = (numbers[:LIST_ROWS] * 256.0 + numbers[LIST_ROWS:]).astype(jnp.int32)
    lists_copy = pltpu.make_async_copy(lists_v, lists_s, sems.at[3])
    lists_copy.start()
    lists_copy.wait()
    wait_all(copies[1:])
    attention(False, lists_s, q_s, kv, result, lse, scores)
    out[...] = result[...].astype(jnp.bfloat16)


def attend_far(letter, recv):
    return pl.pallas_call(
        attend_far_kernel,
        out_shape=(
            jax.ShapeDtypeStruct((ROWS * QROWS, DH), jnp.bfloat16),
            jax.ShapeDtypeStruct((TEAMS, LANES), jnp.float32),
        ),
        in_specs=[ANY] * 2,
        out_specs=(VMEM, VMEM),
        scratch_shapes=[
            LISTS,
            pltpu.VMEM((LIST_ROWS, DH), jnp.int32),
            pltpu.VMEM((2 * LIST_ROWS, DH), jnp.bfloat16),
            QUERIES,
            pages_scratch(RECV),
            RESULT,
            SCORES,
            pltpu.SemaphoreType.DMA((4,)),
        ],
        compiler_params=PARAMS,
        cost_estimate=pl.CostEstimate(flops=10**11, bytes_accessed=10**8, transcendentals=10**6),
        name="attend_far",
    )(letter, recv)


SHIFTS = (2, 1, 3, 0)
BLOCK = 512


def column_tile(place, side, shift, weight):
    y = lax.rem(place[0] + shift, 4)
    z = place[1] if side == 0 else 1 - place[1]
    return weight.at[:, pl.ds(pl.multiple_of((y * 2 + z) * BLOCK, BLOCK), BLOCK)]


def start_tiles(place, side, weight, w, w_sems):
    loads = [
        pltpu.make_async_copy(column_tile(place, side, shift, weight), w.at[n], w_sems.at[n])
        for n, shift in enumerate(SHIFTS)
    ]
    for load in loads:
        load.start()
    return loads


def project(loads, heads, w, outs, terms, out_sems):
    stores = []
    for n, load in enumerate(loads):
        load.wait()
        terms[n] = jnp.dot(heads[...], w[n], preferred_element_type=jnp.float32).astype(jnp.bfloat16)
        store = pltpu.make_async_copy(terms.at[n], outs[n], out_sems.at[n])
        store.start()
        stores.append(store)
    for store in stores:
        store.wait()


TILES = len(SHIFTS)
TERMS = (jax.ShapeDtypeStruct((STEPS * ROWS, BLOCK), jnp.bfloat16),) * TILES
PROJECT_SCRATCH = [
    pltpu.VMEM((TILES, GROUPS * DH, BLOCK), jnp.bfloat16),
    pltpu.VMEM((TILES, STEPS * ROWS, BLOCK), jnp.bfloat16),
    pltpu.SemaphoreType.DMA((TILES,)),
    pltpu.SemaphoreType.DMA((TILES,)),
]


def finish_kernel(place, lists, q, recv, o1, lse1, o2, lse2, weight, heads, *refs):
    outs, refs = refs[:TILES], refs[TILES:]
    lists_s, q_s, kv, o1_s, lse1_s, o2_s, lse2_s, lse3, result, scores, sems, part_sems, w, terms, w_sems, out_sems = refs
    copies = start_all([(lists, lists_s), (q, q_s), (recv, kv.at[pl.ds(1, RECV)])], sems)
    parts = start_all([(lse1, lse1_s), (lse2, lse2_s), (o1, o1_s), (o2, o2_s)], part_sems)
    kv[0] = blank_page()
    wait_all(copies)
    loads = start_tiles(place, 1, weight, w, w_sems)
    attention(False, lists_s, q_s, kv, result, lse3, scores)
    wait_all(parts)

    top = jnp.maximum(jnp.maximum(lse1_s[...], lse2_s[...]), lse3[...])
    parts = [jnp.exp(x[...] - top) for x in (lse1_s, lse2_s, lse3)]
    inverse = 1.0 / (parts[0] + parts[1] + parts[2])
    f1, f2, f3 = [(x * inverse).T for x in parts]
    size = TEAM * GROUPS
    for t in range(STEPS):
        for g in range(TEAMS):
            rows = pl.ds((t * TEAMS + g) * size, size)
            lanes = slice(t * size, (t + 1) * size)
            merged = f1[lanes, g : g + 1] * o1_s[rows, :] + f2[lanes, g : g + 1] * o2_s[rows, :].astype(jnp.float32)
            result[rows, :] = merged + f3[lanes, g : g + 1] * result[rows, :]
        for h in range(GROUPS):
            column = result[pl.ds(t * ROWS * GROUPS + h, ROWS, stride=GROUPS), :]
            heads[pl.ds(t * ROWS, ROWS), pl.ds(h * DH, DH)] = column.astype(jnp.bfloat16)
    project(loads, heads, w, outs, terms, out_sems)


def finish(place, lists, q, recv, o1, lse1, o2, lse2, weight):
    heads = jax.ShapeDtypeStruct((STEPS * ROWS, GROUPS * DH), jnp.bfloat16)
    heads, *terms = pl.pallas_call(
        finish_kernel,
        out_shape=(heads,) + TERMS,
        in_specs=[SMEM] + [ANY] * 8,
        out_specs=(VMEM,) + (ANY,) * TILES,
        scratch_shapes=[
            LISTS, QUERIES, pages_scratch(RECV), RESULT, LSE, QUERIES, LSE, LSE, RESULT, SCORES,
            pltpu.SemaphoreType.DMA((3,)),
            pltpu.SemaphoreType.DMA((4,)),
        ] + PROJECT_SCRATCH,
        compiler_params=PARAMS,
        name="attend_merge_project",
    )(place, lists, q, recv, o1, lse1, o2, lse2, weight)
    return heads, terms


def project_kernel(place, heads, weight, *refs):
    outs, (w, terms, w_sems, out_sems) = refs[:TILES], refs[TILES:]
    project(start_tiles(place, 0, weight, w, w_sems), heads, w, outs, terms, out_sems)


def project_mine(place, heads, weight):
    return pl.pallas_call(
        project_kernel,
        out_shape=TERMS,
        in_specs=[SMEM, VMEM, ANY],
        out_specs=(ANY,) * TILES,
        scratch_shapes=PROJECT_SCRATCH,
        compiler_params=PARAMS,
        cost_estimate=pl.CostEstimate(flops=10**9, bytes_accessed=6 * 10**6, transcendentals=0),
        name="project_mine",
    )(place, heads, weight)


def sum_over_y(terms):
    total = terms[SHIFTS.index(0)].astype(jnp.float32)
    for term, shift in zip(terms, SHIFTS):
        if shift:
            moved = lax.ppermute(term, "ty", [(i, (i + shift) % 4) for i in range(4)])
            total = total + moved.astype(jnp.float32)
    return total


def page_lists(here, place, lengths, fresh=None):
    column = jnp.arange(MAXP, dtype=jnp.int32)[None, :]
    here = here & (column * PAGE < lengths[:, None])
    kept = here.astype(jnp.int32)
    rank = jnp.cumsum(kept, axis=1) - 1
    slot = jnp.arange(MAXP, dtype=jnp.int32)[None, :, None]
    chosen = here[:, None, :] & (rank[:, None, :] == slot)
    idx = jnp.sum(jnp.where(chosen, place[:, None, :], 0), axis=2)
    count = jnp.sum(kept, axis=1)
    tokens = jnp.sum(kept * jnp.minimum(PAGE, lengths[:, None] - column * PAGE), axis=1)
    if fresh is not None:
        idx = jnp.concatenate([fresh, idx], axis=1)
        count, tokens = count + 1, tokens + PAGE
    idx = jnp.pad(idx, ((0, 0), (0, POSITIONS - idx.shape[1])))
    wide = count > NARROW
    place_of = jnp.cumsum(wide.astype(jnp.int32)) - 1
    row = jnp.arange(ROWS, dtype=jnp.int32)
    picked = wide[None, :] & (place_of[None, :] == row[:, None])
    wide_rows = jnp.sum(jnp.where(picked, row[None, :], 0), axis=1)
    wide_count = jnp.broadcast_to(jnp.sum(wide.astype(jnp.int32)), (ROWS,))
    spare = jnp.zeros((LIST_ROWS * DH - LIST,), jnp.int32)
    return jnp.concatenate([idx.reshape(-1), count, tokens, wide_rows, wide_count, spare]).reshape(LIST_ROWS, DH)


def local_lists(table, lengths):
    fresh = 1 + POOL + jnp.arange(ROWS, dtype=jnp.int32)[:, None]
    return page_lists(table < POOL, 1 + table, lengths, fresh)


def arrived_lists(table, lengths, half):
    prompt = table < POOL + N_INST * PCAP
    px, mx = table - POOL, table - (POOL + N_INST * PCAP)
    source = jnp.where(prompt, px // PCAP, mx // MCAP)
    rank = jnp.where(prompt, px % PCAP, PCAP + mx % MCAP)
    group = (source >> 3) * 4 + (source & 3)
    here = (table >= POOL) & (((source >> 2) & 1) == half)
    return page_lists(here, 1 + group * SLOTS + rank, lengths)


def as_rows(lists):
    return jnp.concatenate([lists >> 8, lists & 255], axis=0).astype(jnp.bfloat16)


def per_device(
    queries,
    new_keys,
    new_values,
    pool_keys,
    pool_values,
    prompt_keys,
    prompt_values,
    moved_keys,
    moved_values,
    prompt_dest,
    moved_dest,
    block_table,
    context_len,
    out_weight,
):
    page = lambda x: x.reshape(x.shape[0], PAGE, DH)
    swap = [(0, 1), (1, 0)]
    half = lax.axis_index("izh")

    def exchange(send):
        send = send.reshape(N_HALF, SLOTS, 2, PAGE, DH)
        recv = lax.all_to_all(send, HALF, split_axis=0, concat_axis=0, tiled=True)
        return recv.reshape(RECV, 2, PAGE, DH)

    pages = (page(prompt_keys), page(prompt_values), page(moved_keys), page(moved_values))
    far_recv = exchange(pack((1 - half)[None], prompt_dest, moved_dest, *pages))
    q = queries.reshape(ROWS * QROWS, DH)
    letter = jnp.concatenate([q, as_rows(arrived_lists(block_table, context_len, 1 - half))], axis=0)
    near_lists = arrived_lists(block_table, context_len, half)
    near_send = pack(half[None], prompt_dest, moved_dest, *pages, near_lists)
    fresh = jnp.stack([new_keys, new_values], axis=0).reshape(2, STEPS, ROWS, DH).transpose(2, 0, 1, 3)
    fresh = jnp.pad(fresh, ((0, 0), (0, 0), (0, PAGE - STEPS), (0, 0)))
    local_pages = (page(pool_keys), page(pool_values), fresh)
    local = local_lists(block_table, context_len)
    o1, lse1 = attend_local(local, q, *local_pages, near_send)
    letter = lax.ppermute(gate(letter, lse1), "izh", swap)
    near_recv = exchange(near_send)

    o2, lse2 = attend_far(letter, far_recv)
    o2 = lax.ppermute(o2, "izh", swap)
    lse2 = lax.ppermute(lse2, "izh", swap)

    place = jnp.stack([lax.axis_index("ty"), lax.axis_index("tz")]).astype(jnp.int32)
    heads, terms = finish(place, near_lists, q, near_recv, o1, lse1, o2, lse2, out_weight)
    other = lax.ppermute(sum_over_y(terms).astype(jnp.bfloat16), "tz", swap)
    mine = sum_over_y(project_mine(place, heads, out_weight))
    return (mine + other.astype(jnp.float32)).astype(jnp.bfloat16).reshape(STEPS, ROWS, -1)


def solution(mesh):
    fine = Mesh(mesh.devices.reshape(SIZES), NAMES)
    in_specs = (
        P(None, INST, TP, None),
        P(None, INST, TP, None),
        P(None, INST, TP, None),
        P(INST, TP, None, None),
        P(INST, TP, None, None),
        P(INST, TP, None, None),
        P(INST, TP, None, None),
        P(INST, TP, None, None),
        P(INST, TP, None, None),
        P(INST),
        P(INST),
        P(INST, None),
        P(INST),
        P(TP, None),
    )
    return jax.shard_map(
        per_device, mesh=fine, in_specs=in_specs, out_specs=P(None, INST, TP), check_vma=False
    )
```

```python
import functools

import jax
import jax.numpy as jnp
from jax import lax
from jax.experimental import pallas as pl
from jax.experimental.pallas import tpu as pltpu
from jax.sharding import Mesh, PartitionSpec as P

NAMES = ("ix", "izh", "izl", "ic", "ty", "tz")
SIZES = (4, 2, 2, 2, 4, 2)
INST = ("ix", "izh", "izl", "ic")
HALF = ("ix", "izl", "ic")
TP = ("ty", "tz")

N_INST = 32
N_HALF = 16
STEPS, ROWS, GROUPS, DH = 4, 64, 8, 128
QROWS = STEPS * GROUPS
PAGE, MAXP = 16, 48
POOL, OUT, MIG = 192, 192, 96
PCAP, MCAP = 12, 6
SLOTS = PCAP + MCAP
RECV = N_HALF * SLOTS
NARROW = 8
WIDE = 16
WIDE_CHUNKS = 4
POSITIONS = WIDE * WIDE_CHUNKS
LIST = ROWS * (POSITIONS + 4)
LIST_ROWS = 40
PIECES = 6
TEAM = 4
TEAMS = ROWS // TEAM
LANES = TEAM * QROWS
SCALE = DH ** -0.5
VMEM_LIMIT = 62 * 1024 * 1024

SMEM = pl.BlockSpec(memory_space=pltpu.SMEM)
VMEM = pl.BlockSpec(memory_space=pltpu.VMEM)
ANY = pl.BlockSpec(memory_space=pl.ANY)
PARAMS = pltpu.CompilerParams(vmem_limit_bytes=VMEM_LIMIT)


def start_all(pairs, sems):
    copies = [pltpu.make_async_copy(src, dst, sems.at[n]) for n, (src, dst) in enumerate(pairs)]
    for copy in copies:
        copy.start()
    return copies


def wait_all(copies):
    for copy in copies:
        copy.wait()


def pack_kernel(half, pdest, mdest, pk, pv, mk, mv, *refs):
    out, pages, send, pdest_s, mdest_s, chosen, prompts, moved, sems, out_sems = refs[-10:]
    loads = start_all(
        [
            (pdest, pdest_s),
            (mdest, mdest_s),
            (pk, pages.at[pl.ds(0, OUT), 0]),
            (pv, pages.at[pl.ds(0, OUT), 1]),
            (mk, pages.at[pl.ds(OUT, MIG), 0]),
            (mv, pages.at[pl.ds(OUT, MIG), 1]),
        ],
        sems,
    )
    wanted = half[0]
    for d in range(N_INST):
        prompts[d] = 0
        moved[d] = PCAP

    def clear(n, carry):
        chosen[n] = 0
        return carry

    lax.fori_loop(0, RECV, clear, 0, unroll=8)
    wait_all(loads[:2])

    def rank(dest, count, first, j):
        d = dest[j]
        k = count[d]
        count[d] = k + 1
        group = (d >> 3) * 4 + (d & 3)
        chosen[jnp.where(((d >> 2) & 1) == wanted, group * SLOTS + k, RECV)] = first + j

    def copy_page(n, carry):
        send[n] = pages[chosen[n]]
        return carry

    def ranks(j, carry):
        rank(pdest_s, prompts, 0, 2 * j)
        rank(mdest_s, moved, OUT, j)
        rank(pdest_s, prompts, 0, 2 * j + 1)
        return carry

    lax.fori_loop(0, MIG, ranks, 0, unroll=8)
    wait_all(loads[2:])
    stores = []
    for n in range(PIECES):
        piece = pl.ds(n * (RECV // PIECES), RECV // PIECES)
        lax.fori_loop(n * (RECV // PIECES), (n + 1) * (RECV // PIECES), copy_page, 0, unroll=8)
        stores += start_all([(send.at[piece], out.at[piece])], out_sems.at[pl.ds(n, 1)])
    wait_all(stores)


def pack(half, pdest, mdest, pk, pv, mk, mv, *after):
    return pl.pallas_call(
        pack_kernel,
        out_shape=jax.ShapeDtypeStruct((RECV, 2, PAGE, DH), jnp.bfloat16),
        in_specs=[SMEM] + [ANY] * (6 + len(after)),
        out_specs=ANY,
        scratch_shapes=[
            pltpu.VMEM((OUT + MIG, 2, PAGE, DH), jnp.bfloat16),
            pltpu.VMEM((RECV, 2, PAGE, DH), jnp.bfloat16),
            pltpu.SMEM((OUT,), jnp.int32),
            pltpu.SMEM((MIG,), jnp.int32),
            pltpu.SMEM((RECV + 1,), jnp.int32),
            pltpu.SMEM((N_INST,), jnp.int32),
            pltpu.SMEM((N_INST,), jnp.int32),
            pltpu.SemaphoreType.DMA((6,)),
            pltpu.SemaphoreType.DMA((PIECES,)),
        ],
        compiler_params=PARAMS,
        cost_estimate=pl.CostEstimate(flops=10**6, bytes_accessed=10**7, transcendentals=0),
        name="pack_pages",
    )(half, pdest, mdest, pk, pv, mk, mv, *after)


def gate_kernel(x, *refs):
    pass


def gate(x, *after):
    return pl.pallas_call(
        gate_kernel,
        out_shape=jax.ShapeDtypeStruct(x.shape, x.dtype),
        in_specs=[ANY] * (1 + len(after)),
        out_specs=ANY,
        input_output_aliases={0: 0},
        name="gate",
    )(x, *after)


def attention(fresh, lists, q, kv, out, lse, scores):
    lane = lax.broadcasted_iota(jnp.int32, (1, LANES), 1)
    team_row = (lane // GROUPS) % TEAM
    step = lane // (TEAM * GROUPS)

    def entry(i):
        return lists[i // DH, i % DH] if isinstance(i, int) else lists[i >> 7, i & 127]

    def load(r, first, n, which):
        return [kv[entry(r * POSITIONS + first + p), which] for p in range(n)]

    def count(r):
        return entry(ROWS * POSITIONS + r)

    def tokens(r):
        return entry(ROWS * (POSITIONS + 1) + r)

    def team(t, g):
        first = t * ROWS * GROUPS + g * TEAM * GROUPS
        return pl.ds(first if isinstance(g, int) else pl.multiple_of(first, TEAM * GROUPS), TEAM * GROUPS)

    def queries(g):
        return jnp.concatenate([q[team(t, g), :] for t in range(STEPS)], axis=0)

    def mask(s, first, limit):
        token = lax.broadcasted_iota(jnp.int32, s.shape, 0) + first
        seen = token < limit
        if fresh:
            seen = token < jnp.where(token < PAGE, step + 1, limit)
        return jnp.where(seen, s * SCALE, -jnp.inf)

    def dot_nt(a, b):
        return lax.dot_general(a, b, (((1,), (1,)), ((), ())), preferred_element_type=jnp.float32)

    def narrow(g):
        width = NARROW * PAGE
        rows = [g * TEAM + i for i in range(TEAM)]
        keys = jnp.concatenate([k for r in rows for k in load(r, 0, NARROW, 0)], axis=0)
        s_all = dot_nt(keys, queries(g))
        s = s_all[:width]
        limit = jnp.full((1, LANES), tokens(rows[0]), jnp.int32)
        owner = (lax.broadcasted_iota(jnp.int32, (width, LANES), 1) // GROUPS) % TEAM
        for i in range(1, TEAM):
            s = jnp.where(owner == i, s_all[i * width : (i + 1) * width], s)
            limit = jnp.where(team_row == i, tokens(rows[i]), limit)
        s = mask(s, 0, limit)
        m = jnp.maximum(jnp.max(s, axis=0, keepdims=True), -1e30)
        e = jnp.exp(s - m)
        total = jnp.sum(e, axis=0, keepdims=True)
        safe = jnp.maximum(total, 1e-30)
        lse[pl.ds(g, 1), :] = jnp.where(total > 0.0, m + jnp.log(safe), -1e30)
        weights = (e * (1.0 / safe)).T
        for i in range(TEAM):
            values = jnp.concatenate(load(rows[i], 0, NARROW, 1), axis=0)
            pieces = [weights[(t * TEAM + i) * GROUPS : (t * TEAM + i + 1) * GROUPS] for t in range(STEPS)]
            part = jnp.concatenate(pieces, axis=0).astype(jnp.bfloat16)
            product = jnp.dot(part, values, preferred_element_type=jnp.float32)
            for t in range(STEPS):
                first = (t * ROWS + rows[i]) * GROUPS
                out[pl.ds(first, GROUPS), :] = product[t * GROUPS : (t + 1) * GROUPS]

    for g in range(TEAMS):
        narrow(g)

    def put(r, product, m, total, safe):
        g, i = r // TEAM, r % TEAM
        size = TEAM * GROUPS
        owner = lax.broadcasted_iota(jnp.int32, (size, DH), 0) // GROUPS
        for t in range(STEPS):
            rows = team(t, g)
            out[rows, :] = jnp.where(owner == i, product[t * size : (t + 1) * size], out[rows, :])
        new = jnp.where(total > 0.0, m + jnp.log(safe), -1e30)
        lse[pl.ds(g, 1), :] = jnp.where(team_row == i, new, lse[pl.ds(g, 1), :])

    def chunk_scores(r, c):
        keys = jnp.concatenate(load(r, c * WIDE, WIDE, 0), axis=0)
        return mask(dot_nt(keys, queries(r // TEAM)), c * WIDE * PAGE, tokens(r))

    def chunk_out(r, c, weights):
        values = jnp.concatenate(load(r, c * WIDE, WIDE, 1), axis=0)
        return jnp.dot(weights.T.astype(jnp.bfloat16), values, preferred_element_type=jnp.float32)

    def one_chunk(r):
        s = chunk_scores(r, 0)
        m = jnp.maximum(jnp.max(s, axis=0, keepdims=True), -1e30)
        e = jnp.exp(s - m)
        total = jnp.sum(e, axis=0, keepdims=True)
        safe = jnp.maximum(total, 1e-30)
        put(r, chunk_out(r, 0, e * (1.0 / safe)), m, total, safe)

    def more_chunks(r):
        chunks = (count(r) + WIDE - 1) // WIDE

        def first_pass(c, m):
            s = chunk_scores(r, c)
            scores[c] = s
            return jnp.maximum(m, jnp.max(s, axis=0, keepdims=True))

        m = lax.fori_loop(0, chunks, first_pass, jnp.full((1, LANES), -1e30, jnp.float32))

        def second_pass(c, total):
            e = jnp.exp(scores[c] - m)
            scores[c] = e
            return total + jnp.sum(e, axis=0, keepdims=True)

        total = lax.fori_loop(0, chunks, second_pass, jnp.zeros((1, LANES), jnp.float32))
        safe = jnp.maximum(total, 1e-30)
        inverse = 1.0 / safe

        def third_pass(c, product):
            return product + chunk_out(r, c, scores[c] * inverse)

        product = lax.fori_loop(0, chunks, third_pass, jnp.zeros((LANES, DH), jnp.float32))
        put(r, product, m, total, safe)

    def wide_body(k, carry):
        r = entry(ROWS * (POSITIONS + 2) + k)
        pl.when(count(r) <= WIDE)(lambda: one_chunk(r))
        pl.when(count(r) > WIDE)(lambda: more_chunks(r))
        return carry

    lax.fori_loop(0, entry(ROWS * (POSITIONS + 3)), wide_body, 0)


QUERIES = pltpu.VMEM((ROWS * QROWS, DH), jnp.bfloat16)
SCORES = pltpu.VMEM((WIDE_CHUNKS, WIDE * PAGE, LANES), jnp.float32)
RESULT = pltpu.VMEM((ROWS * QROWS, DH), jnp.float32)
LSE = pltpu.VMEM((TEAMS, LANES), jnp.float32)
LISTS = pltpu.SMEM((LIST_ROWS, DH), jnp.int32)


def pages_scratch(n):
    return pltpu.VMEM((1 + n, 2, PAGE, DH), jnp.bfloat16)


def blank_page():
    return jnp.zeros((2, PAGE, DH), jnp.bfloat16)


def attend_local_kernel(lists, q, pool_k, pool_v, fresh, after, out, lse, lists_s, q_s, kv, scores, sems):
    copies = start_all(
        [
            (lists, lists_s),
            (q, q_s),
            (pool_k, kv.at[pl.ds(1, POOL), 0]),
            (pool_v, kv.at[pl.ds(1, POOL), 1]),
            (fresh, kv.at[pl.ds(1 + POOL, ROWS)]),
        ],
        sems,
    )
    kv[0] = blank_page()
    wait_all(copies)
    attention(True, lists_s, q_s, kv, out, lse, scores)


def attend_local(lists, q, pool_k, pool_v, fresh, after):
    return pl.pallas_call(
        attend_local_kernel,
        out_shape=(
            jax.ShapeDtypeStruct((ROWS * QROWS, DH), jnp.float32),
            jax.ShapeDtypeStruct((TEAMS, LANES), jnp.float32),
        ),
        in_specs=[ANY] * 6,
        out_specs=(VMEM, VMEM),
        scratch_shapes=[LISTS, QUERIES, pages_scratch(POOL + ROWS), SCORES, pltpu.SemaphoreType.DMA((5,))],
        compiler_params=PARAMS,
        cost_estimate=pl.CostEstimate(flops=10**11, bytes_accessed=10**8, transcendentals=10**6),
        name="attend_local",
    )(lists, q, pool_k, pool_v, fresh, after)


def attend_far_kernel(letter, recv, out, lse, lists_s, lists_v, coded, q_s, kv, result, scores, sems):
    copies = start_all(
        [
            (letter.at[pl.ds(ROWS * QROWS, 2 * LIST_ROWS)], coded),
            (letter.at[pl.ds(0, ROWS * QROWS)], q_s),
            (recv, kv.at[pl.ds(1, RECV)]),
        ],
        sems,
    )
    kv[0] = blank_page()
    copies[0].wait()
    numbers = coded[...].astype(jnp.float32)
    lists_v[...] = (numbers[:LIST_ROWS] * 256.0 + numbers[LIST_ROWS:]).astype(jnp.int32)
    lists_copy = pltpu.make_async_copy(lists_v, lists_s, sems.at[3])
    lists_copy.start()
    lists_copy.wait()
    wait_all(copies[1:])
    attention(False, lists_s, q_s, kv, result, lse, scores)
    out[...] = result[...].astype(jnp.bfloat16)


def attend_far(letter, recv):
    return pl.pallas_call(
        attend_far_kernel,
        out_shape=(
            jax.ShapeDtypeStruct((ROWS * QROWS, DH), jnp.bfloat16),
            jax.ShapeDtypeStruct((TEAMS, LANES), jnp.float32),
        ),
        in_specs=[ANY] * 2,
        out_specs=(VMEM, VMEM),
        scratch_shapes=[
            LISTS,
            pltpu.VMEM((LIST_ROWS, DH), jnp.int32),
            pltpu.VMEM((2 * LIST_ROWS, DH), jnp.bfloat16),
            QUERIES,
            pages_scratch(RECV),
            RESULT,
            SCORES,
            pltpu.SemaphoreType.DMA((4,)),
        ],
        compiler_params=PARAMS,
        cost_estimate=pl.CostEstimate(flops=10**11, bytes_accessed=10**8, transcendentals=10**6),
        name="attend_far",
    )(letter, recv)


SHIFTS = (2, 1, 3, 0)
BLOCK = 512


def column_tile(place, side, shift, weight):
    y = lax.rem(place[0] + shift, 4)
    z = place[1] if side == 0 else 1 - place[1]
    return weight.at[:, pl.ds(pl.multiple_of((y * 2 + z) * BLOCK, BLOCK), BLOCK)]


def start_tiles(place, side, weight, w, w_sems):
    loads = [
        pltpu.make_async_copy(column_tile(place, side, shift, weight), w.at[n], w_sems.at[n])
        for n, shift in enumerate(SHIFTS)
    ]
    for load in loads:
        load.start()
    return loads


def project(loads, heads, w, outs, terms, out_sems):
    stores = []
    for n, load in enumerate(loads):
        load.wait()
        terms[n] = jnp.dot(heads[...], w[n], preferred_element_type=jnp.float32).astype(jnp.bfloat16)
        store = pltpu.make_async_copy(terms.at[n], outs[n], out_sems.at[n])
        store.start()
        stores.append(store)
    for store in stores:
        store.wait()


TILES = len(SHIFTS)
TERMS = (jax.ShapeDtypeStruct((STEPS * ROWS, BLOCK), jnp.bfloat16),) * TILES
PROJECT_SCRATCH = [
    pltpu.VMEM((TILES, GROUPS * DH, BLOCK), jnp.bfloat16),
    pltpu.VMEM((TILES, STEPS * ROWS, BLOCK), jnp.bfloat16),
    pltpu.SemaphoreType.DMA((TILES,)),
    pltpu.SemaphoreType.DMA((TILES,)),
]


def finish_kernel(place, lists, q, recv, o1, lse1, o2, lse2, weight, heads_out, *refs):
    outs, refs = refs[:TILES], refs[TILES:]
    lists_s, q_s, kv, o1_s, lse1_s, o2_s, lse2_s, lse3, result, scores, heads, sems, part_sems, heads_sem, w, terms, w_sems, out_sems = refs
    copies = start_all([(lists, lists_s), (q, q_s), (recv, kv.at[pl.ds(1, RECV)])], sems)
    parts = start_all([(lse1, lse1_s), (lse2, lse2_s), (o1, o1_s), (o2, o2_s)], part_sems)
    kv[0] = blank_page()
    wait_all(copies)
    loads = start_tiles(place, 1, weight, w, w_sems)
    attention(False, lists_s, q_s, kv, result, lse3, scores)
    wait_all(parts)

    top = jnp.maximum(jnp.maximum(lse1_s[...], lse2_s[...]), lse3[...])
    parts = [jnp.exp(x[...] - top) for x in (lse1_s, lse2_s, lse3)]
    inverse = 1.0 / (parts[0] + parts[1] + parts[2])
    f1, f2, f3 = [(x * inverse).T for x in parts]
    size = TEAM * GROUPS
    for t in range(STEPS):
        for g in range(TEAMS):
            rows = pl.ds((t * TEAMS + g) * size, size)
            lanes = slice(t * size, (t + 1) * size)
            merged = f1[lanes, g : g + 1] * o1_s[rows, :] + f2[lanes, g : g + 1] * o2_s[rows, :].astype(jnp.float32)
            result[rows, :] = merged + f3[lanes, g : g + 1] * result[rows, :]
        for h in range(GROUPS):
            column = result[pl.ds(t * ROWS * GROUPS + h, ROWS, stride=GROUPS), :]
            heads[pl.ds(t * ROWS, ROWS), pl.ds(h * DH, DH)] = column.astype(jnp.bfloat16)
    heads_store = start_all([(heads, heads_out)], heads_sem)
    project(loads, heads, w, outs, terms, out_sems)
    wait_all(heads_store)


def finish(place, lists, q, recv, o1, lse1, o2, lse2, weight):
    heads = jax.ShapeDtypeStruct((STEPS * ROWS, GROUPS * DH), jnp.bfloat16)
    heads, *terms = pl.pallas_call(
        finish_kernel,
        out_shape=(heads,) + TERMS,
        in_specs=[SMEM] + [ANY] * 8,
        out_specs=(ANY,) * (1 + TILES),
        scratch_shapes=[
            LISTS, QUERIES, pages_scratch(RECV), RESULT, LSE, QUERIES, LSE, LSE, RESULT, SCORES,
            pltpu.VMEM((STEPS * ROWS, GROUPS * DH), jnp.bfloat16),
            pltpu.SemaphoreType.DMA((3,)),
            pltpu.SemaphoreType.DMA((4,)),
            pltpu.SemaphoreType.DMA((1,)),
        ] + PROJECT_SCRATCH,
        compiler_params=PARAMS,
        name="attend_merge_project",
    )(place, lists, q, recv, o1, lse1, o2, lse2, weight)
    return heads, terms


def project_kernel(place, heads, weight, *refs):
    outs, (w, terms, w_sems, out_sems) = refs[:TILES], refs[TILES:]
    project(start_tiles(place, 0, weight, w, w_sems), heads, w, outs, terms, out_sems)


def project_mine(place, heads, weight):
    return pl.pallas_call(
        project_kernel,
        out_shape=TERMS,
        in_specs=[SMEM, VMEM, ANY],
        out_specs=(ANY,) * TILES,
        scratch_shapes=PROJECT_SCRATCH,
        compiler_params=PARAMS,
        cost_estimate=pl.CostEstimate(flops=10**9, bytes_accessed=6 * 10**6, transcendentals=0),
        name="project_mine",
    )(place, heads, weight)


def sum_over_y(terms):
    total = terms[SHIFTS.index(0)].astype(jnp.float32)
    for term, shift in zip(terms, SHIFTS):
        if shift:
            moved = lax.ppermute(term, "ty", [(i, (i + shift) % 4) for i in range(4)])
            total = total + moved.astype(jnp.float32)
    return total


def page_lists(here, place, lengths, fresh=None):
    column = jnp.arange(MAXP, dtype=jnp.int32)[None, :]
    here = here & (column * PAGE < lengths[:, None])
    kept = here.astype(jnp.int32)
    rank = jnp.cumsum(kept, axis=1) - 1
    slot = jnp.arange(MAXP, dtype=jnp.int32)[None, :, None]
    chosen = here[:, None, :] & (rank[:, None, :] == slot)
    idx = jnp.sum(jnp.where(chosen, place[:, None, :], 0), axis=2)
    count = jnp.sum(kept, axis=1)
    tokens = jnp.sum(kept * jnp.minimum(PAGE, lengths[:, None] - column * PAGE), axis=1)
    if fresh is not None:
        idx = jnp.concatenate([fresh, idx], axis=1)
        count, tokens = count + 1, tokens + PAGE
    idx = jnp.pad(idx, ((0, 0), (0, POSITIONS - idx.shape[1])))
    wide = count > NARROW
    place_of = jnp.cumsum(wide.astype(jnp.int32)) - 1
    row = jnp.arange(ROWS, dtype=jnp.int32)
    picked = wide[None, :] & (place_of[None, :] == row[:, None])
    wide_rows = jnp.sum(jnp.where(picked, row[None, :], 0), axis=1)
    wide_count = jnp.broadcast_to(jnp.sum(wide.astype(jnp.int32)), (ROWS,))
    spare = jnp.zeros((LIST_ROWS * DH - LIST,), jnp.int32)
    return jnp.concatenate([idx.reshape(-1), count, tokens, wide_rows, wide_count, spare]).reshape(LIST_ROWS, DH)


def local_lists(table, lengths):
    fresh = 1 + POOL + jnp.arange(ROWS, dtype=jnp.int32)[:, None]
    return page_lists(table < POOL, 1 + table, lengths, fresh)


def arrived_lists(table, lengths, half):
    prompt = table < POOL + N_INST * PCAP
    px, mx = table - POOL, table - (POOL + N_INST * PCAP)
    source = jnp.where(prompt, px // PCAP, mx // MCAP)
    rank = jnp.where(prompt, px % PCAP, PCAP + mx % MCAP)
    group = (source >> 3) * 4 + (source & 3)
    here = (table >= POOL) & (((source >> 2) & 1) == half)
    return page_lists(here, 1 + group * SLOTS + rank, lengths)


def as_rows(lists):
    return jnp.concatenate([lists >> 8, lists & 255], axis=0).astype(jnp.bfloat16)


def per_device(
    queries,
    new_keys,
    new_values,
    pool_keys,
    pool_values,
    prompt_keys,
    prompt_values,
    moved_keys,
    moved_values,
    prompt_dest,
    moved_dest,
    block_table,
    context_len,
    out_weight,
):
    page = lambda x: x.reshape(x.shape[0], PAGE, DH)
    swap = [(0, 1), (1, 0)]
    half = lax.axis_index("izh")

    def exchange(send):
        send = send.reshape(N_HALF, SLOTS, 2, PAGE, DH)
        recv = lax.all_to_all(send, HALF, split_axis=0, concat_axis=0, tiled=True)
        return recv.reshape(RECV, 2, PAGE, DH)

    pages = (page(prompt_keys), page(prompt_values), page(moved_keys), page(moved_values))
    far_recv = exchange(pack((1 - half)[None], prompt_dest, moved_dest, *pages))
    q = queries.reshape(ROWS * QROWS, DH)
    letter = jnp.concatenate([q, as_rows(arrived_lists(block_table, context_len, 1 - half))], axis=0)
    near_lists = arrived_lists(block_table, context_len, half)
    near_send = pack(half[None], prompt_dest, moved_dest, *pages, near_lists)
    fresh = jnp.stack([new_keys, new_values], axis=0).reshape(2, STEPS, ROWS, DH).transpose(2, 0, 1, 3)
    fresh = jnp.pad(fresh, ((0, 0), (0, 0), (0, PAGE - STEPS), (0, 0)))
    local_pages = (page(pool_keys), page(pool_values), fresh)
    local = local_lists(block_table, context_len)
    o1, lse1 = attend_local(local, q, *local_pages, near_send)
    letter = lax.ppermute(gate(letter, lse1), "izh", swap)
    near_recv = exchange(near_send)

    o2, lse2 = attend_far(letter, far_recv)
    o2 = lax.ppermute(o2, "izh", swap)
    lse2 = lax.ppermute(lse2, "izh", swap)

    place = jnp.stack([lax.axis_index("ty"), lax.axis_index("tz")]).astype(jnp.int32)
    heads, terms = finish(place, near_lists, q, near_recv, o1, lse1, o2, lse2, out_weight)
    other = lax.ppermute(sum_over_y(terms).astype(jnp.bfloat16), "tz", swap)
    mine = sum_over_y(project_mine(place, heads, out_weight))
    return (mine + other.astype(jnp.float32)).astype(jnp.bfloat16).reshape(STEPS, ROWS, -1)


def solution(mesh):
    fine = Mesh(mesh.devices.reshape(SIZES), NAMES)
    in_specs = (
        P(None, INST, TP, None),
        P(None, INST, TP, None),
        P(None, INST, TP, None),
        P(INST, TP, None, None),
        P(INST, TP, None, None),
        P(INST, TP, None, None),
        P(INST, TP, None, None),
        P(INST, TP, None, None),
        P(INST, TP, None, None),
        P(INST),
        P(INST),
        P(INST, None),
        P(INST),
        P(TP, None),
    )
    return jax.shard_map(
        per_device, mesh=fine, in_specs=in_specs, out_specs=P(None, INST, TP), check_vma=False
    )
```
